32 devices in a mesh: row: 8 (over z, x), col: 4 (over y, core).
Axes of the slice: x: 2, y: 2, z: 4, core: 2. Of those that a mesh axis runs over, the one named last changes fastest.
Arguments:
- activations: bfloat16 [512, 12288], P('col', 'row'), may hold values from -6 to 6
- weight_tiles: bfloat16 [4, 8, 12, 4096], P('col', 'row'), may hold values from -0.125 to 0.125
- tile_ids: int32 [4, 8, 12], P('col', 'row'), may hold values from 0 to 2303, as said below
- tile_counts: int32 [4, 8], P('col', 'row'), may hold values from 7 to 12, as said below
- upstream: bfloat16 [512, 24576], P('col', 'row'), may hold values from -0.119628906 to 0.119628906
Outputs:
- output: bfloat16 [512, 24576], P('col', 'row')
- weight_grad: bfloat16 [4, 8, 12, 4096], P('col', 'row')
The draws below stay inside these ranges and needn't reach their ends.
Inputs may be any that keep to these rules, and one draw needn't show every extreme that they name: `tile_ids`: within one block the 12 slots name distinct tiles; only slots below the block's count are used. `tile_counts`: some block is full in every draw.
All inputs are finite; a program needn't handle non-finite values.
Results may differ from the reference program's by a relative error of at most 0.017.
Values may be sent and summed in bfloat16 or wider, within the bound.
A program may use at most 64 MiB of HBM per device.

```python
import jax
import jax.numpy as jnp
from jax import lax

D = 12288
FF = 24576
TILE = 64
CAP = 12
TOK_DEV = 128
TOK = 512
TPB = 2304
N_ROW = 8
N_COL = 4


def pick_tiles(block_key):
    return jax.random.permutation(block_key, TPB)[:CAP]


def draw_tile_ids(key, part):
    keys = jax.random.split(key, N_COL * N_ROW)
    chosen = jax.vmap(pick_tiles)(keys)
    return chosen.reshape(N_COL, N_ROW, CAP).astype(jnp.int32)


def draw_tile_counts(key, part):
    counts = jax.random.randint(key, (N_COL * N_ROW,), CAP // 2 + 1, CAP + 1)
    place = jax.random.randint(jax.random.fold_in(key, 7), (), 0, N_COL * N_ROW)
    counts = jnp.where(jnp.arange(N_COL * N_ROW) == place, CAP, counts)
    return counts.reshape(N_COL, N_ROW).astype(jnp.int32)


def steps_of(rng, shape, pieces, least, largest):
    factor_of, own = 1.0, jax.random.fold_in(rng, 6)
    for dim, blocks in pieces:
        draws = jnp.exp(jax.random.uniform(jax.random.fold_in(own, dim), (blocks,), jnp.float32, least / len(pieces), largest / len(pieces)))
        factor_of = factor_of * jnp.repeat(draws, shape[dim] // blocks).reshape([-1 if axis == dim else 1 for axis in range(len(shape))])
    return factor_of


def gaussian(stream_key, dims, spread, bound, pieces=(), kind=jnp.bfloat16):
    entries = spread * jax.random.normal(stream_key, dims, jnp.float32)
    if pieces:
        entries = entries * steps_of(stream_key, dims, pieces, -0.22, 0.18)
    return jnp.clip(entries, -bound, bound).astype(kind)


def setup_inputs(seed: int = 0) -> dict:
    streams_of = jax.random.split(jax.random.key(seed), 6)
    activations = gaussian(streams_of[0], (TOK, D), 1.0, 6.0, ((0, 4), (1, 8)))
    weight_tiles = gaussian(streams_of[1], (N_COL, N_ROW, CAP, TILE * TILE), (D // 5) ** -0.5, 0.125, ((0, 4), (1, 8)))
    tile_ids = draw_tile_ids(jax.random.fold_in(streams_of[5], 71), 0)
    tile_counts = draw_tile_counts(jax.random.fold_in(streams_of[5], 71), 0)
    upstream = gaussian(streams_of[4], (TOK, FF), 0.02, 0.119628906, ((0, 4), (1, 8)))
    return dict(activations=activations, weight_tiles=weight_tiles, tile_ids=tile_ids, tile_counts=tile_counts, upstream=upstream)


def gelu_parts(pre):
    cumul = 0.5 * (1.0 + jax.scipy.special.erf(pre * 0.7071067811865476))
    density = jnp.exp(-0.5 * pre * pre) * 0.3989422804014327
    return cumul, density


def reference(activations, weight_tiles, tile_ids, tile_counts, upstream):
    d_block = D // N_COL // TILE
    per_col = FF // N_ROW // TILE
    ff_local = FF // N_ROW
    slots = N_COL * CAP
    x_all = activations.reshape(TOK, D // TILE, TILE)
    owner = jnp.arange(slots, dtype=jnp.int32) // CAP
    position = jnp.arange(slots, dtype=jnp.int32) % CAP

    def one_block(index):
        tiles = lax.dynamic_index_in_dim(weight_tiles, index, 1, keepdims=False)
        tiles = tiles.reshape(slots, TILE, TILE).astype(jnp.float32)
        slot_ids = lax.dynamic_index_in_dim(tile_ids, index, 1, keepdims=False).reshape(slots).astype(jnp.int32)
        counts_col = lax.dynamic_index_in_dim(tile_counts, index, 1, keepdims=False).astype(jnp.int32)
        live = position < counts_col[owner]
        d_tile = (owner * d_block + slot_ids // per_col).astype(jnp.int32)
        f_tile = (slot_ids % per_col).astype(jnp.int32)
        placing = ((f_tile[:, None] == jnp.arange(per_col, dtype=jnp.int32)[None, :]) & live[:, None]).astype(jnp.float32)
        x_tiles = jnp.take(x_all, d_tile, axis=1).astype(jnp.float32)
        partial_value = jnp.einsum("tsk,skn->tsn", x_tiles, tiles)
        pre = jnp.einsum("tsn,sf->tfn", partial_value, placing, precision=lax.Precision.HIGHEST).reshape(TOK, ff_local)
        cumul, density = gelu_parts(pre)
        output = (pre * cumul).astype(jnp.bfloat16)
        up_block = lax.dynamic_slice_in_dim(upstream, index * ff_local, ff_local, 1).astype(jnp.float32)
        grad_pre = (up_block * (cumul + pre * density)).astype(jnp.bfloat16)
        g_tiles = jnp.take(grad_pre.reshape(TOK, per_col, TILE), f_tile, axis=1).astype(jnp.float32)
        groups = jnp.einsum("gtsk,gtsn->gskn", x_tiles.reshape(N_COL, TOK_DEV, slots, TILE), g_tiles.reshape(N_COL, TOK_DEV, slots, TILE))
        rounded = lax.optimization_barrier(groups.astype(jnp.bfloat16)).astype(jnp.float32)
        summed = jnp.sum(rounded, axis=0).reshape(N_COL, CAP, TILE * TILE)
        grad = jnp.where(live.reshape(N_COL, CAP)[:, :, None], summed, 0.0).astype(jnp.bfloat16)
        return output, grad

    outputs, grads = lax.map(one_block, jnp.arange(N_ROW, dtype=jnp.int32))
    output = jnp.transpose(outputs, (1, 0, 2)).reshape(TOK, FF)
    weight_grad = jnp.transpose(grads, (1, 0, 2, 3))
    return (output, weight_grad)
```

```python
import functools

import jax
import jax.numpy as jnp
from jax import lax
from jax.experimental import pallas as pl
from jax.experimental.pallas import tpu as pltpu
from jax.sharding import PartitionSpec as P

TILE = 64
LANES = 128
MESH = pl.DeviceIdType.MESH


def gelu_parts(pre):
    cumul = 0.5 * (1.0 + lax.erf(pre * 0.7071067811865476))
    density = jnp.exp(-0.5 * pre * pre) * 0.3989422804014327
    return (cumul, density)


def kernel(
    n_row, n_col, per_col,
    xt_ref, w_ref, ids_ref, cnt_ref, up_ref, out_ref, grad_ref,
    xg, sendx, recvx, wbuf, idsrc, idq, idc, sidq, sidc, pre, prod, g, dsend, drecv,
    xg_s, xg_r, ic_s, ic_r, iq_s, iq_r, w_s, w_r, xz_s, xz_r, d_s, d_r, loc,
):
    cap = ids_ref.shape[0]
    half = cap // 2
    group = n_row // n_col
    line = n_col
    own_tiles = xt_ref.shape[0]
    n_pair = pre.shape[0]
    col = lax.axis_index("col")
    row = lax.axis_index("row")
    z = row // group
    x = lax.rem(row, group)

    def member(k):
        return lax.rem(x + k, group)

    def at_line(k):
        return lax.rem(z + k, line)

    def at_col(k):
        return lax.rem(col + k, n_col)

    barrier = pltpu.get_barrier_semaphore()
    for k in range(1, group):
        pl.semaphore_signal(barrier, inc=1, device_id={"row": z * group + member(k)}, device_id_type=MESH)
    for k in range(1, line):
        pl.semaphore_signal(barrier, inc=1, device_id={"row": at_line(k) * group + x}, device_id_type=MESH)
    for k in range(1, n_col):
        pl.semaphore_signal(barrier, inc=1, device_id={"col": at_col(k)}, device_id_type=MESH)

    lane8 = lax.broadcasted_iota(jnp.int32, (8, LANES), 1)
    packed = jnp.where(lane8 == cap, cnt_ref[0], 0)
    for s in range(cap):
        packed = jnp.where(lane8 == s, ids_ref[s], packed)
    idsrc[...] = packed
    idc[col] = packed
    wbuf[col] = w_ref[...]
    pl.semaphore_wait(barrier, group + line + n_col - 3)

    def remote(src, dst, send, recv, target):
        return pltpu.make_async_remote_copy(
            src_ref=src, dst_ref=dst, send_sem=send, recv_sem=recv, device_id=target, device_id_type=MESH
        )

    def ids_col(k, owner):
        return remote(idsrc, idc.at[owner], ic_s.at[k], ic_r.at[owner], {"col": at_col(k)})

    def ids_line(k, owner):
        to = at_line(k)
        return remote(idc.at[to], idq.at[owner], iq_s.at[k], iq_r.at[owner], {"row": to * group + x})

    def w_col(k, owner):
        return remote(w_ref, wbuf.at[owner], w_s.at[k], w_r.at[owner], {"col": at_col(k)})

    def x_group(k, owner):
        return remote(
            xt_ref, xg.at[pl.ds(owner * own_tiles, own_tiles)], xg_s.at[k], xg_r.at[owner],
            {"row": z * group + member(k)},
        )

    def x_line(k, owner):
        to = at_line(k)
        return remote(sendx.at[to], recvx.at[owner], xz_s.at[k], xz_r.at[owner], {"row": to * group + x})

    def d_col(k, owner):
        to = at_col(k)
        return remote(dsend.at[to], drecv.at[owner], d_s.at[k], d_r.at[owner], {"col": to})

    for k in range(1, n_col):
        ids_col(k, col).start()
    for k in range(1, group):
        x_group(k, x).start()
    for k in range(1, n_col):
        w_col(k, col).start()
    xg[pl.ds(x * own_tiles, own_tiles)] = xt_ref[...]

    for k in range(1, n_col):
        ids_col(k, at_col(k)).wait_recv()
    for k in range(1, line):
        ids_line(k, z).start()
    idq[z] = idc[z]
    pre[...] = jnp.zeros_like(pre)
    for k in range(1, line):
        ids_line(k, at_line(k)).wait_recv()
    copy_q = pltpu.make_async_copy(idq, sidq, loc.at[0])
    copy_c = pltpu.make_async_copy(idc, sidc, loc.at[1])
    copy_q.start()
    copy_c.start()
    copy_q.wait()
    copy_c.wait()

    for k in range(1, group):
        x_group(k, member(k)).wait_recv()
    for k in range(line - 1, 0, -1):
        to = at_line(k)
        for s in range(cap):
            sendx[to, s] = xg[sidq[to, 0, s] // per_col]
        x_line(k, z).start()
    for s in range(cap):
        recvx[z, s] = xg[sidq[z, 0, s] // per_col]
    for k in range(1, n_col):
        w_col(k, at_col(k)).wait_recv()

    lane_half = lax.broadcasted_iota(jnp.int32, (TILE, LANES), 1) // TILE

    def add_block(b):
        count = sidc[b, 0, cap]
        places = []
        for s in range(cap):
            f = lax.rem(sidc[b, 0, s], per_col)
            places.append(jnp.where(s < count, f // 2, -1))
            both = jnp.where(lane_half == s // half, wbuf[b, s % half].astype(jnp.float32), 0.0)
            both = both + pltpu.roll(both, TILE, 1)
            placed = jnp.where(lane_half == lax.rem(f, 2), both, 0.0).astype(jnp.bfloat16)
            prod[s] = lax.dot_general(
                recvx[b, s], placed, (((0,), (0,)), ((), ())), preferred_element_type=jnp.float32
            )

        def add_pair(p, carry):
            total = pre[p]
            for s in range(cap):
                total = total + prod[s] * jnp.where(places[s] == p, 1.0, 0.0)
            pre[p] = total
            return carry

        lax.fori_loop(0, n_pair, add_pair, 0)

    add_block(z)

    def later_block(k, carry):
        b = at_line(k)
        x_line(k, b).wait_recv()
        add_block(b)
        return carry

    lax.fori_loop(1, line, later_block, 0)

    for p in range(n_pair):
        lanes = slice(p * LANES, (p + 1) * LANES)
        v = pre[p]
        cumul, density = gelu_parts(v)
        out_ref[:, lanes] = (v * cumul).astype(jnp.bfloat16)
        g[p] = (up_ref[:, lanes].astype(jnp.float32) * (cumul + v * density)).astype(jnp.bfloat16)

    def terms(b):
        for j in range(half):
            parts = []
            for s in (j, j + half):
                f = lax.rem(sidc[b, 0, s], per_col)
                r = jnp.dot(recvx[b, s], g[f // 2], preferred_element_type=jnp.float32)
                r = jnp.where(lane_half == lax.rem(f, 2), r, 0.0)
                parts.append(r + pltpu.roll(r, TILE, 1))
            dsend[b, j] = jnp.where(lane_half == 0, parts[0], parts[1]).astype(jnp.bfloat16)

    def send_terms(k, carry):
        terms(at_col(k))
        d_col(k, col).start()
        return carry

    lax.fori_loop(1, n_col, send_terms, 0)
    terms(col)
    for k in range(1, n_col):
        d_col(k, at_col(k)).wait_recv()
    own_count = cnt_ref[0]
    for j in range(half):
        total = dsend[col, j].astype(jnp.float32)
        for k in range(1, n_col):
            total = total + drecv[at_col(k), j].astype(jnp.float32)
        grad_ref[j] = jnp.where(lane_half * half + j < own_count, total, 0.0).astype(jnp.bfloat16)

    for k in range(1, group):
        x_group(k, x).wait_send()
    for k in range(1, line):
        ids_line(k, z).wait_send()
        x_line(k, z).wait_send()
    for k in range(1, n_col):
        ids_col(k, col).wait_send()
        w_col(k, col).wait_send()
        d_col(k, col).wait_send()


def body(activations, weight_tiles, tile_ids, tile_counts, upstream):
    n_row, n_col = lax.axis_size("row"), lax.axis_size("col")
    group = n_row // n_col
    tok, own_width = activations.shape
    ff_local = upstream.shape[1]
    per_col = ff_local // TILE
    cap = weight_tiles.shape[2]
    half = cap // 2
    own_tiles = own_width // TILE
    xt = activations.T.reshape(own_tiles, TILE, tok)
    w = weight_tiles.reshape(2, half, TILE, TILE).transpose(1, 2, 0, 3).reshape(half, TILE, 2 * TILE)
    bf16, f32, i32 = jnp.bfloat16, jnp.float32, jnp.int32
    vmem = pl.BlockSpec(memory_space=pltpu.VMEM)
    smem = pl.BlockSpec(memory_space=pltpu.SMEM)
    dma = pltpu.SemaphoreType.DMA
    n_pair = ff_local // LANES
    output, grad = pl.pallas_call(
        functools.partial(kernel, n_row, n_col, per_col),
        out_shape=(
            jax.ShapeDtypeStruct((tok, ff_local), bf16),
            jax.ShapeDtypeStruct((half, TILE, LANES), bf16),
        ),
        in_specs=[vmem, vmem, smem, smem, vmem],
        out_specs=(vmem, vmem),
        scratch_shapes=[
            pltpu.VMEM((group * own_tiles, TILE, tok), bf16),
            pltpu.VMEM((n_col, cap, TILE, tok), bf16),
            pltpu.VMEM((n_col, cap, TILE, tok), bf16),
            pltpu.VMEM((n_col, half, TILE, LANES), bf16),
            pltpu.VMEM((8, LANES), i32),
            pltpu.VMEM((n_col, 8, LANES), i32),
            pltpu.VMEM((n_col, 8, LANES), i32),
            pltpu.SMEM((n_col, 8, LANES), i32),
            pltpu.SMEM((n_col, 8, LANES), i32),
            pltpu.VMEM((n_pair, tok, LANES), f32),
            pltpu.VMEM((cap, tok, LANES), f32),
            pltpu.VMEM((n_pair, tok, LANES), bf16),
            pltpu.VMEM((n_col, half, TILE, LANES), bf16),
            pltpu.VMEM((n_col, half, TILE, LANES), bf16),
            dma((group,)), dma((group,)),
            dma((n_col,)), dma((n_col,)),
            dma((n_col,)), dma((n_col,)),
            dma((n_col,)), dma((n_col,)),
            dma((n_col,)), dma((n_col,)),
            dma((n_col,)), dma((n_col,)),
            dma((2,)),
        ],
        compiler_params=pltpu.CompilerParams(
            collective_id=0, has_side_effects=True, vmem_limit_bytes=40 * 1024 * 1024
        ),
    )(xt, w, tile_ids.reshape(cap), tile_counts.reshape(1), upstream)
    grad = grad.reshape(half, TILE, 2, TILE).transpose(2, 0, 1, 3)
    return (output, grad.reshape(1, 1, cap, TILE * TILE))


def solution(mesh):
    return jax.shard_map(
        body,
        mesh=mesh,
        in_specs=(
            P("col", "row"),
            P("col", "row", None, None),
            P("col", "row", None),
            P("col", "row"),
            P("col", "row"),
        ),
        out_specs=(P("col", "row"), P("col", "row", None, None)),
        check_vma=False,
    )
```

```python
import functools

import jax
import jax.numpy as jnp
from jax import lax
from jax.experimental import pallas as pl
from jax.experimental.pallas import tpu as pltpu
from jax.sharding import PartitionSpec as P

TILE = 64
LANES = 128
CHUNKS = 4
UNROLL = 3
MESH = pl.DeviceIdType.MESH


def gelu_parts(pre):
    cumul = 0.5 * (1.0 + lax.erf(pre * 0.7071067811865476))
    density = jnp.exp(-0.5 * pre * pre) * 0.3989422804014327
    return (cumul, density)


def kernel(
    n_row, n_col, per_col,
    x_ref, w_ref, ids_ref, cnt_ref, up_ref, out_ref, grad_ref, *scratch,
):
    xg, scratch = scratch[:CHUNKS], scratch[CHUNKS:]
    (
        sendx, recvx, wbuf, wpl, idsrc, idq, idc, sidq, sidc, table, stable, prod, run, g, dw, dsend, drecv,
        xg_s, xg_r, ic_s, ic_r, iq_s, iq_r, w_s, w_r, xz_s, xz_r, d_s, d_r, loc,
    ) = scratch
    cap = ids_ref.shape[0]
    half = cap // 2
    slots = n_col * cap
    group = n_row // n_col
    line = n_col
    chunks = len(xg)
    all_tiles, packed_rows, _ = xg[0].shape
    tc = 2 * packed_rows
    own_tiles = all_tiles // group
    n_pair = g.shape[0]
    col = lax.axis_index("col")
    row = lax.axis_index("row")
    z = row // group
    x = lax.rem(row, group)

    def member(k):
        return lax.rem(x + k, group)

    def at_line(k):
        return lax.rem(z + k, line)

    def at_col(k):
        return lax.rem(col + k, n_col)

    barrier = pltpu.get_barrier_semaphore()
    for k in range(1, group):
        pl.semaphore_signal(barrier, inc=1, device_id={"row": z * group + member(k)}, device_id_type=MESH)
    for k in range(1, line):
        pl.semaphore_signal(barrier, inc=1, device_id={"row": at_line(k) * group + x}, device_id_type=MESH)
    for k in range(1, n_col):
        pl.semaphore_signal(barrier, inc=1, device_id={"col": at_col(k)}, device_id_type=MESH)

    lane8 = lax.broadcasted_iota(jnp.int32, (8, LANES), 1)
    packed = jnp.where(lane8 == cap, cnt_ref[0], 0)
    for s in range(cap):
        packed = jnp.where(lane8 == s, ids_ref[s], packed)
    idsrc[...] = packed
    idc[col] = packed
    wbuf[col] = w_ref[...]

    def pack(c):
        for t in range(own_tiles):
            lanes = slice(t * TILE, (t + 1) * TILE)
            top = x_ref[c * tc : c * tc + packed_rows, lanes].astype(jnp.float32)
            bottom = x_ref[c * tc + packed_rows : (c + 1) * tc, lanes].astype(jnp.float32)
            xg[c][x * own_tiles + t] = jnp.concatenate([top, bottom], axis=1).astype(jnp.bfloat16)

    pack(0)
    pl.semaphore_wait(barrier, group + line + n_col - 3)

    def remote(src, dst, send, recv, target):
        return pltpu.make_async_remote_copy(
            src_ref=src, dst_ref=dst, send_sem=send, recv_sem=recv, device_id=target, device_id_type=MESH
        )

    def ids_col(k, owner):
        return remote(idsrc, idc.at[owner], ic_s.at[k], ic_r.at[owner], {"col": at_col(k)})

    def ids_line(k, owner):
        to = at_line(k)
        return remote(idc.at[to], idq.at[owner], iq_s.at[k], iq_r.at[owner], {"row": to * group + x})

    def w_col(k, owner):
        return remote(w_ref, wbuf.at[owner], w_s.at[k], w_r.at[owner], {"col": at_col(k)})

    def x_group(c, k, owner):
        mine = xg[c].at[pl.ds(x * own_tiles, own_tiles)]
        theirs = xg[c].at[pl.ds(owner * own_tiles, own_tiles)]
        return remote(mine, theirs, xg_s.at[c, k], xg_r.at[c, owner], {"row": z * group + member(k)})

    def x_line(c, k, owner):
        to = at_line(k)
        return remote(
            sendx.at[c, to], recvx.at[c, owner], xz_s.at[c, k], xz_r.at[c, owner], {"row": to * group + x}
        )

    def d_col(k, owner):
        to = at_col(k)
        return remote(dsend.at[to], drecv.at[owner], d_s.at[k], d_r.at[owner], {"col": to})

    for k in range(1, n_col):
        ids_col(k, col).start()
    for k in range(1, group):
        x_group(0, k, x).start()
    for k in range(1, n_col):
        w_col(k, col).start()
    for c in range(1, chunks):
        pack(c)
        for k in range(1, group):
            x_group(c, k, x).start()

    for k in range(1, n_col):
        ids_col(k, at_col(k)).wait_recv()
    for k in range(1, line):
        ids_line(k, z).start()
    idq[z] = idc[z]
    copy_c = pltpu.make_async_copy(idc, sidc, loc.at[1])
    copy_c.start()
    for k in range(1, line):
        ids_line(k, at_line(k)).wait_recv()
    copy_q = pltpu.make_async_copy(idq, sidq, loc.at[0])
    copy_q.start()
    copy_c.wait()
    copy_q.wait()

    for c in range(chunks):
        for k in range(1, group):
            x_group(c, k, member(k)).wait_recv()
        for k in range(line - 1, 0, -1):
            to = at_line(k)
            for s in range(cap):
                sendx[c, to, s] = xg[c][sidq[to, 0, s] // per_col]
            x_line(c, k, z).start()
        for s in range(cap):
            recvx[c, z, s] = xg[c][sidq[z, 0, s] // per_col]

    width = table.shape[1]
    lanes_s = lax.broadcasted_iota(jnp.int32, (slots, width), 1)
    rows_s = lax.broadcasted_iota(jnp.int32, (slots, width), 0)
    key_row = jnp.full((1, width), per_col + 1, jnp.int32) * slots + slots
    key_col = jnp.zeros((slots, width), jnp.int32)
    lane1 = lax.broadcasted_iota(jnp.int32, (1, width), 1)
    for s in range(slots):
        b, j = s // cap, s % cap
        f = jnp.where(j < sidc[b, 0, cap], lax.rem(sidc[b, 0, j], per_col), per_col)
        key_row = jnp.where(lane1 == s, f * slots + s, key_row)
        key_col = jnp.where(rows_s == s, f, key_col)
    ahead = jnp.where(key_row < key_col * slots + rows_s, 1, 0)
    rank = jnp.sum(ahead, axis=1, keepdims=True)
    here = jnp.where(rank == lanes_s, 1, 0)
    table[0:1, :] = jnp.sum(here * rows_s, axis=0, keepdims=True)
    table[1:2, :] = jnp.sum(here * key_col, axis=0, keepdims=True)
    upto = jnp.sum(jnp.where(key_col <= lanes_s, 1, 0), axis=0, keepdims=True)
    some = jnp.sum(jnp.where(key_col == lanes_s, 1, 0), axis=0, keepdims=True)
    table[2:3, :] = jnp.where(some > 0, upto - 1, slots)
    table[3:8, :] = jnp.zeros((5, width), jnp.int32)
    copy_t = pltpu.make_async_copy(table, stable, loc.at[0])
    copy_t.start()
    copy_t.wait()

    for k in range(1, n_col):
        w_col(k, at_col(k)).wait_recv()

    lane_half = lax.broadcasted_iota(jnp.int32, (TILE, LANES), 1) // TILE

    def place_weights(b, carry):
        for s in range(cap):
            f = lax.rem(sidc[b, 0, s], per_col)
            both = jnp.where(lane_half == s // half, wbuf[b, s % half].astype(jnp.float32), 0.0)
            both = both + pltpu.roll(both, TILE, 1)
            placed = jnp.where(lane_half == lax.rem(f, 2), both, 0.0).astype(jnp.bfloat16)
            wpl[b * cap + s, :TILE] = placed
            wpl[b * cap + s, TILE:] = placed
        return carry

    lax.fori_loop(0, n_col, place_weights, 0)
    run[slots] = jnp.zeros((tc, LANES), jnp.float32)

    packed_half = lax.broadcasted_iota(jnp.int32, (packed_rows, LANES), 1) // TILE
    first = jnp.where(packed_half == 0, 1.0, 0.0).astype(jnp.bfloat16)
    second = jnp.where(packed_half == 1, 1.0, 0.0).astype(jnp.bfloat16)

    def spread(c, b, s):
        tile = recvx[c, b, s]
        return jnp.concatenate([tile * first, tile * second], axis=0)

    def products(c, b):
        for s in range(cap):
            prod[b * cap + s] = jnp.dot(spread(c, b, s), wpl[b * cap + s], preferred_element_type=jnp.float32)

    def hidden(c):
        products(c, z)

        def later(k, carry):
            b = at_line(k)
            x_line(c, k, b).wait_recv()
            products(c, b)
            return carry

        lax.fori_loop(1, line, later, 0)

        def add_run(r, held):
            same = jnp.where(stable[1, r] == stable[1, jnp.maximum(r - 1, 0)], 1.0, 0.0)
            total = prod[stable[0, r]] + held * same
            run[r] = total
            return total

        lax.fori_loop(0, slots, add_run, jnp.zeros((tc, LANES), jnp.float32), unroll=4)

        rows = pl.ds(pl.multiple_of(c * tc, tc), tc)

        def gelu_pair(p, carry):
            lanes = pl.ds(pl.multiple_of(p * LANES, LANES), LANES)
            v = run[stable[2, 2 * p]] + run[stable[2, 2 * p + 1]]
            cumul, density = gelu_parts(v)
            out_ref[rows, lanes] = (v * cumul).astype(jnp.bfloat16)
            g[p] = (up_ref[rows, lanes].astype(jnp.float32) * (cumul + v * density)).astype(jnp.bfloat16)
            return carry

        lax.fori_loop(0, n_pair, gelu_pair, 0, unroll=UNROLL)

    def add_terms(c, b, first_chunk):
        for s in range(cap):
            f = lax.rem(sidc[b, 0, s], per_col)
            r = lax.dot_general(
                spread(c, b, s), g[f // 2], (((0,), (0,)), ((), ())), preferred_element_type=jnp.float32
            )
            term = r[:TILE] + r[TILE:]
            dw[b * cap + s] = term if first_chunk else dw[b * cap + s] + term

    def round_terms(b):
        for j in range(half):
            parts = []
            for s in (j, j + half):
                f = lax.rem(sidc[b, 0, s], per_col)
                r = jnp.where(lane_half == lax.rem(f, 2), dw[b * cap + s], 0.0)
                parts.append(r + pltpu.roll(r, TILE, 1))
            dsend[b, j] = jnp.where(lane_half == 0, parts[0], parts[1]).astype(jnp.bfloat16)

    def all_terms(c, first_chunk):
        def one(b, carry):
            add_terms(c, b, first_chunk)
            return carry

        lax.fori_loop(0, n_col, one, 0)

    hidden(0)
    if chunks > 1:
        all_terms(0, True)

        def middle(c, carry):
            hidden(c)
            all_terms(c, False)
            return carry

        lax.fori_loop(1, chunks - 1, middle, 0)
        hidden(chunks - 1)

    def send_terms(i, carry):
        k = 1 + lax.rem(n_col // 2 - 1 + i, n_col - 1)
        b = at_col(k)
        add_terms(chunks - 1, b, chunks == 1)
        round_terms(b)
        d_col(k, col).start()
        return carry

    lax.fori_loop(0, n_col - 1, send_terms, 0)
    add_terms(chunks - 1, col, chunks == 1)
    round_terms(col)
    for k in range(1, n_col):
        d_col(k, at_col(k)).wait_recv()
    own_count = cnt_ref[0]
    for j in range(half):
        total = dsend[col, j].astype(jnp.float32)
        for k in range(1, n_col):
            total = total + drecv[at_col(k), j].astype(jnp.float32)
        grad_ref[j] = jnp.where(lane_half * half + j < own_count, total, 0.0).astype(jnp.bfloat16)

    for c in range(chunks):
        for k in range(1, group):
            x_group(c, k, x).wait_send()
        for k in range(1, line):
            x_line(c, k, z).wait_send()
    for k in range(1, line):
        ids_line(k, z).wait_send()
    for k in range(1, n_col):
        ids_col(k, col).wait_send()
        w_col(k, col).wait_send()
        d_col(k, col).wait_send()


def body(activations, weight_tiles, tile_ids, tile_counts, upstream):
    n_row, n_col = lax.axis_size("row"), lax.axis_size("col")
    group = n_row // n_col
    tok, own_width = activations.shape
    ff_local = upstream.shape[1]
    per_col = ff_local // TILE
    cap = weight_tiles.shape[2]
    half = cap // 2
    slots = n_col * cap
    own_tiles = own_width // TILE
    tc = tok // CHUNKS
    rows = tc // 2
    width = -(-max(slots, per_col) // LANES) * LANES
    w = weight_tiles.reshape(2, half, TILE, TILE).transpose(1, 2, 0, 3).reshape(half, TILE, 2 * TILE)
    bf16, f32, i32 = jnp.bfloat16, jnp.float32, jnp.int32
    vmem = pl.BlockSpec(memory_space=pltpu.VMEM)
    smem = pl.BlockSpec(memory_space=pltpu.SMEM)
    dma = pltpu.SemaphoreType.DMA
    n_pair = ff_local // LANES
    output, grad = pl.pallas_call(
        functools.partial(kernel, n_row, n_col, per_col),
        out_shape=(
            jax.ShapeDtypeStruct((tok, ff_local), bf16),
            jax.ShapeDtypeStruct((half, TILE, LANES), bf16),
        ),
        in_specs=[vmem, vmem, smem, smem, vmem],
        out_specs=(vmem, vmem),
        scratch_shapes=[
            *[pltpu.VMEM((group * own_tiles, rows, LANES), bf16) for _ in range(CHUNKS)],
            pltpu.VMEM((CHUNKS, n_col, cap, rows, LANES), bf16),
            pltpu.VMEM((CHUNKS, n_col, cap, rows, LANES), bf16),
            pltpu.VMEM((n_col, half, TILE, LANES), bf16),
            pltpu.VMEM((slots, 2 * TILE, LANES), bf16),
            pltpu.VMEM((8, LANES), i32),
            pltpu.VMEM((n_col, 8, LANES), i32),
            pltpu.VMEM((n_col, 8, LANES), i32),
            pltpu.SMEM((n_col, 8, LANES), i32),
            pltpu.SMEM((n_col, 8, LANES), i32),
            pltpu.VMEM((8, width), i32),
            pltpu.SMEM((8, width), i32),
            pltpu.VMEM((slots, tc, LANES), f32),
            pltpu.VMEM((slots + 1, tc, LANES), f32),
            pltpu.VMEM((n_pair, tc, LANES), bf16),
            pltpu.VMEM((slots, TILE, LANES), f32),
            pltpu.VMEM((n_col, half, TILE, LANES), bf16),
            pltpu.VMEM((n_col, half, TILE, LANES), bf16),
            dma((CHUNKS, group)), dma((CHUNKS, group)),
            dma((n_col,)), dma((n_col,)),
            dma((n_col,)), dma((n_col,)),
            dma((n_col,)), dma((n_col,)),
            dma((CHUNKS, n_col)), dma((CHUNKS, n_col)),
            dma((n_col,)), dma((n_col,)),
            dma((2,)),
        ],
        compiler_params=pltpu.CompilerParams(
            collective_id=0, has_side_effects=True, vmem_limit_bytes=48 * 1024 * 1024
        ),
    )(activations, w, tile_ids.reshape(cap), tile_counts.reshape(1), upstream)
    grad = grad.reshape(half, TILE, 2, TILE).transpose(2, 0, 1, 3)
    return (output, grad.reshape(1, 1, cap, TILE * TILE))


def solution(mesh):
    return jax.shard_map(
        body,
        mesh=mesh,
        in_specs=(
            P("col", "row"),
            P("col", "row", None, None),
            P("col", "row", None),
            P("col", "row"),
            P("col", "row"),
        ),
        out_specs=(P("col", "row"), P("col", "row", None, None)),
        check_vma=False,
    )
```

```python
import functools

import jax
import jax.numpy as jnp
from jax import lax
from jax.experimental import pallas as pl
from jax.experimental.pallas import tpu as pltpu
from jax.sharding import PartitionSpec as P

TILE = 64
LANES = 128
CHUNKS = 4
UNROLL = 3
MESH = pl.DeviceIdType.MESH


def gelu_parts(pre):
    cumul = 0.5 * (1.0 + lax.erf(pre * 0.7071067811865476))
    density = jnp.exp(-0.5 * pre * pre) * 0.3989422804014327
    return (cumul, density)


def kernel(
    n_row, n_col, per_col,
    x_hbm, w_ref, ids_ref, cnt_ref, up_hbm, out_ref, grad_ref, *scratch,
):
    xg, scratch = scratch[:CHUNKS], scratch[CHUNKS:]
    (
        x_ref, up_ref, natural, mixed, wsrc, sendx, recvx, wbuf, wpl, xall, idsrc, idq, idc, sidq, sidc, table, stable,
        prod, run, g, gt, dsend, drecv,
        xg_s, xg_r, ic_s, ic_r, iq_s, iq_r, w_s, w_r, xz_s, xz_r, d_s, d_r, loc,
    ) = scratch
    cap = ids_ref.shape[0]
    half = cap // 2
    slots = n_col * cap
    group = n_row // n_col
    line = n_col
    chunks = len(xg)
    all_tiles, packed_rows, _ = xg[0].shape
    tc = 2 * packed_rows
    own_tiles = all_tiles // group
    n_pair = g.shape[0]
    col = lax.axis_index("col")
    row = lax.axis_index("row")
    z = row // group
    x = lax.rem(row, group)

    def member(k):
        return lax.rem(x + k, group)

    def at_line(k):
        return lax.rem(z + k, line)

    def at_col(k):
        return lax.rem(col + k, n_col)

    copy_x = pltpu.make_async_copy(x_hbm, x_ref, loc.at[2])
    copy_up = pltpu.make_async_copy(up_hbm, up_ref, loc.at[3])
    copy_x.start()
    copy_up.start()
    barrier = pltpu.get_barrier_semaphore()
    for k in range(1, group):
        pl.semaphore_signal(barrier, inc=1, device_id={"row": z * group + member(k)}, device_id_type=MESH)
    for k in range(1, line):
        pl.semaphore_signal(barrier, inc=1, device_id={"row": at_line(k) * group + x}, device_id_type=MESH)
    for k in range(1, n_col):
        pl.semaphore_signal(barrier, inc=1, device_id={"col": at_col(k)}, device_id_type=MESH)

    lane8 = lax.broadcasted_iota(jnp.int32, (8, LANES), 1)
    packed = jnp.where(lane8 == cap, cnt_ref[0], 0)
    for s in range(cap):
        packed = jnp.where(lane8 == s, ids_ref[s], packed)
    idsrc[...] = packed
    idc[col] = packed

    def pack(c):
        for t in range(own_tiles):
            lanes = slice(t * TILE, (t + 1) * TILE)
            top = x_ref[c * tc : c * tc + packed_rows, lanes].astype(jnp.float32)
            bottom = x_ref[c * tc + packed_rows : (c + 1) * tc, lanes].astype(jnp.float32)
            xg[c][x * own_tiles + t] = jnp.concatenate([top, bottom], axis=1).astype(jnp.bfloat16)

    copy_x.wait()
    pack(0)
    pl.semaphore_wait(barrier, group + line + n_col - 3)

    def remote(src, dst, send, recv, target):
        return pltpu.make_async_remote_copy(
            src_ref=src, dst_ref=dst, send_sem=send, recv_sem=recv, device_id=target, device_id_type=MESH
        )

    def ids_col(k, owner):
        return remote(idsrc, idc.at[owner], ic_s.at[k], ic_r.at[owner], {"col": at_col(k)})

    def ids_line(k, owner):
        to = at_line(k)
        return remote(idc.at[to], idq.at[owner], iq_s.at[k], iq_r.at[owner], {"row": to * group + x})

    def w_col(k, owner):
        return remote(wsrc, wbuf.at[owner], w_s.at[k], w_r.at[owner], {"col": at_col(k)})

    def x_group(c, k, owner):
        mine = xg[c].at[pl.ds(x * own_tiles, own_tiles)]
        theirs = xg[c].at[pl.ds(owner * own_tiles, own_tiles)]
        return remote(mine, theirs, xg_s.at[c, k], xg_r.at[c, owner], {"row": z * group + member(k)})

    def x_line(c, k, owner):
        to = at_line(k)
        return remote(
            sendx.at[c, to], recvx.at[c, owner], xz_s.at[c, k], xz_r.at[c, owner], {"row": to * group + x}
        )

    def d_col(k, owner):
        to = at_col(k)
        return remote(dsend.at[to], drecv.at[owner], d_s.at[k], d_r.at[owner], {"col": to})

    for k in range(1, n_col):
        ids_col(k, col).start()
    for k in range(1, group):
        x_group(0, k, x).start()
    for c in range(1, chunks):
        pack(c)
        for k in range(1, group):
            x_group(c, k, x).start()

    for k in range(1, n_col):
        ids_col(k, at_col(k)).wait_recv()
    for k in range(1, line):
        ids_line(k, z).start()
    idq[z] = idc[z]
    copy_c = pltpu.make_async_copy(idc, sidc, loc.at[1])
    copy_c.start()

    lane_half = lax.broadcasted_iota(jnp.int32, (TILE, LANES), 1) // TILE
    low = lax.broadcasted_iota(jnp.int32, (TILE // 2, LANES), 1) < TILE
    even, odd = pl.ds(0, TILE // 2, stride=2), pl.ds(1, TILE // 2, stride=2)
    for j in range(TILE // 2):
        natural[:, j, :] = w_ref[:, j * LANES : (j + 1) * LANES].astype(jnp.float32)
    for j in range(half):
        one, two = natural[j], natural[j + half]
        mixed[even, :] = jnp.where(low, one, pltpu.roll(two, TILE, 1))
        mixed[odd, :] = jnp.where(low, pltpu.roll(one, TILE, 1), two)
        wsrc[j] = mixed[...].astype(jnp.bfloat16)
    wbuf[col] = wsrc[...]
    for k in range(1, n_col):
        w_col(k, col).start()

    for k in range(1, line):
        ids_line(k, at_line(k)).wait_recv()
    copy_q = pltpu.make_async_copy(idq, sidq, loc.at[0])
    copy_q.start()
    copy_c.wait()
    copy_q.wait()

    for c in range(chunks):
        for k in range(1, group):
            x_group(c, k, member(k)).wait_recv()
        for k in range(line - 1, 0, -1):
            to = at_line(k)
            for s in range(cap):
                sendx[c, to, s] = xg[c][sidq[to, 0, s] // per_col]
            x_line(c, k, z).start()
        for s in range(cap):
            recvx[c, z, s] = xg[c][sidq[z, 0, s] // per_col]

    width = table.shape[1]
    lanes_s = lax.broadcasted_iota(jnp.int32, (slots, width), 1)
    rows_s = lax.broadcasted_iota(jnp.int32, (slots, width), 0)
    key_row = jnp.full((1, width), per_col + 1, jnp.int32) * slots + slots
    key_col = jnp.zeros((slots, width), jnp.int32)
    lane1 = lax.broadcasted_iota(jnp.int32, (1, width), 1)
    for s in range(slots):
        b, j = s // cap, s % cap
        f = jnp.where(j < sidc[b, 0, cap], lax.rem(sidc[b, 0, j], per_col), per_col)
        key_row = jnp.where(lane1 == s, f * slots + s, key_row)
        key_col = jnp.where(rows_s == s, f, key_col)
    ahead = jnp.where(key_row < key_col * slots + rows_s, 1, 0)
    rank = jnp.sum(ahead, axis=1, keepdims=True)
    here = jnp.where(rank == lanes_s, 1, 0)
    table[0:1, :] = jnp.sum(here * rows_s, axis=0, keepdims=True)
    table[1:2, :] = jnp.sum(here * key_col, axis=0, keepdims=True)
    upto = jnp.sum(jnp.where(key_col <= lanes_s, 1, 0), axis=0, keepdims=True)
    some = jnp.sum(jnp.where(key_col == lanes_s, 1, 0), axis=0, keepdims=True)
    table[2:3, :] = jnp.where(some > 0, upto - 1, slots)
    table[3:8, :] = jnp.zeros((5, width), jnp.int32)
    copy_t = pltpu.make_async_copy(table, stable, loc.at[0])
    copy_t.start()
    copy_t.wait()

    for k in range(1, n_col):
        w_col(k, at_col(k)).wait_recv()

    def place_weights(b, carry):
        for s in range(cap):
            f = lax.rem(sidc[b, 0, s], per_col)
            both = jnp.where(lane_half == s // half, wbuf[b, s % half].astype(jnp.float32), 0.0)
            both = both + pltpu.roll(both, TILE, 1)
            placed = jnp.where(lane_half == lax.rem(f, 2), both, 0.0).astype(jnp.bfloat16)
            wpl[b * cap + s, :TILE] = placed
            wpl[b * cap + s, TILE:] = placed
        return carry

    lax.fori_loop(0, n_col, place_weights, 0)
    run[slots] = jnp.zeros((tc, LANES), jnp.float32)

    packed_half = lax.broadcasted_iota(jnp.int32, (packed_rows, LANES), 1) // TILE
    first = jnp.where(packed_half == 0, 1.0, 0.0).astype(jnp.bfloat16)
    second = jnp.where(packed_half == 1, 1.0, 0.0).astype(jnp.bfloat16)

    def chunk_rows(c):
        return pl.ds(pl.multiple_of(c * tc, tc), tc)

    def products(c, b):
        for s in range(cap):
            tile = recvx[c, b, s]
            spread = jnp.concatenate([tile * first, tile * second], axis=0)
            xall[b * cap + s, chunk_rows(c)] = spread
            prod[b * cap + s] = jnp.dot(spread, wpl[b * cap + s], preferred_element_type=jnp.float32)

    def hidden(c, last):
        products(c, z)

        def later(k, carry):
            b = at_line(k)
            x_line(c, k, b).wait_recv()
            products(c, b)
            return carry

        lax.fori_loop(1, line, later, 0)

        def add_run(r, held):
            same = jnp.where(stable[1, r] == stable[1, jnp.maximum(r - 1, 0)], 1.0, 0.0)
            total = prod[stable[0, r]] + held * same
            run[r] = total
            return total

        lax.fori_loop(0, slots, add_run, jnp.zeros((tc, LANES), jnp.float32), unroll=4)

        rows = chunk_rows(c)

        def gelu_pair(p, carry):
            lanes = pl.ds(pl.multiple_of(p * LANES, LANES), LANES)
            v = run[stable[2, 2 * p]] + run[stable[2, 2 * p + 1]]
            cumul, density = gelu_parts(v)
            out_ref[rows, lanes] = (v * cumul).astype(jnp.bfloat16)
            g[p, rows] = (up_ref[rows, lanes].astype(jnp.float32) * (cumul + v * density)).astype(jnp.bfloat16)
            if last:
                both = g[p].astype(jnp.float32).T.astype(jnp.bfloat16)
                gt[2 * p] = both[:TILE]
                gt[2 * p + 1] = both[TILE:]
            return carry

        lax.fori_loop(0, n_pair, gelu_pair, 0, unroll=UNROLL)

    def terms(b):
        for j in range(half):
            parts = []
            for i in (j, j + half):
                f = lax.rem(sidc[b, 0, i], per_col)
                parts.append(jnp.dot(gt[f], xall[b * cap + i], preferred_element_type=jnp.float32))
            turned = jnp.concatenate(parts, axis=0).T
            dsend[b, j] = (turned[:TILE] + turned[TILE:]).astype(jnp.bfloat16)

    copy_up.wait()

    def early(c, carry):
        hidden(c, False)
        return carry

    lax.fori_loop(0, chunks - 1, early, 0)
    hidden(chunks - 1, True)

    def send_terms(i, carry):
        k = 1 + lax.rem(n_col // 2 - 1 + i, n_col - 1)
        terms(at_col(k))
        d_col(k, col).start()
        return carry

    lax.fori_loop(0, n_col - 1, send_terms, 0)
    terms(col)
    for k in range(1, n_col):
        d_col(k, at_col(k)).wait_recv()
    own_count = cnt_ref[0]
    for j in range(half):
        total = dsend[col, j].astype(jnp.float32)
        for k in range(1, n_col):
            total = total + drecv[at_col(k), j].astype(jnp.float32)
        mixed[...] = jnp.where(lane_half * half + j < own_count, total, 0.0)
        one, two = mixed[even, :], mixed[odd, :]
        natural[j] = jnp.where(low, one, pltpu.roll(two, TILE, 1))
        natural[j + half] = jnp.where(low, pltpu.roll(one, TILE, 1), two)
    for j in range(TILE // 2):
        grad_ref[:, j * LANES : (j + 1) * LANES] = natural[:, j, :].astype(jnp.bfloat16)

    for c in range(chunks):
        for k in range(1, group):
            x_group(c, k, x).wait_send()
        for k in range(1, line):
            x_line(c, k, z).wait_send()
    for k in range(1, line):
        ids_line(k, z).wait_send()
    for k in range(1, n_col):
        ids_col(k, col).wait_send()
        w_col(k, col).wait_send()
        d_col(k, col).wait_send()


def body(activations, weight_tiles, tile_ids, tile_counts, upstream):
    n_row, n_col = lax.axis_size("row"), lax.axis_size("col")
    group = n_row // n_col
    tok, own_width = activations.shape
    ff_local = upstream.shape[1]
    per_col = ff_local // TILE
    cap = weight_tiles.shape[2]
    half = cap // 2
    slots = n_col * cap
    own_tiles = own_width // TILE
    tc = tok // CHUNKS
    rows = tc // 2
    width = -(-max(slots, per_col) // LANES) * LANES
    w = weight_tiles.reshape(cap, TILE * TILE)
    bf16, f32, i32 = jnp.bfloat16, jnp.float32, jnp.int32
    vmem = pl.BlockSpec(memory_space=pltpu.VMEM)
    smem = pl.BlockSpec(memory_space=pltpu.SMEM)
    hbm = pl.BlockSpec(memory_space=pltpu.HBM)
    dma = pltpu.SemaphoreType.DMA
    n_pair = ff_local // LANES
    output, grad = pl.pallas_call(
        functools.partial(kernel, n_row, n_col, per_col),
        out_shape=(
            jax.ShapeDtypeStruct((tok, ff_local), bf16),
            jax.ShapeDtypeStruct((cap, TILE * TILE), bf16),
        ),
        in_specs=[hbm, vmem, smem, smem, hbm],
        out_specs=(vmem, vmem),
        scratch_shapes=[
            *[pltpu.VMEM((group * own_tiles, rows, LANES), bf16) for _ in range(CHUNKS)],
            pltpu.VMEM(activations.shape, bf16),
            pltpu.VMEM(upstream.shape, bf16),
            pltpu.VMEM((cap, TILE // 2, LANES), f32),
            pltpu.VMEM((TILE, LANES), f32),
            pltpu.VMEM((half, TILE, LANES), bf16),
            pltpu.VMEM((CHUNKS, n_col, cap, rows, LANES), bf16),
            pltpu.VMEM((CHUNKS, n_col, cap, rows, LANES), bf16),
            pltpu.VMEM((n_col, half, TILE, LANES), bf16),
            pltpu.VMEM((slots, 2 * TILE, LANES), bf16),
            pltpu.VMEM((slots, tok, LANES), bf16),
            pltpu.VMEM((8, LANES), i32),
            pltpu.VMEM((n_col, 8, LANES), i32),
            pltpu.VMEM((n_col, 8, LANES), i32),
            pltpu.SMEM((n_col, 8, LANES), i32),
            pltpu.SMEM((n_col, 8, LANES), i32),
            pltpu.VMEM((8, width), i32),
            pltpu.SMEM((8, width), i32),
            pltpu.VMEM((slots, tc, LANES), f32),
            pltpu.VMEM((slots + 1, tc, LANES), f32),
            pltpu.VMEM((n_pair, tok, LANES), bf16),
            pltpu.VMEM((per_col, TILE, tok), bf16),
            pltpu.VMEM((n_col, half, TILE, LANES), bf16),
            pltpu.VMEM((n_col, half, TILE, LANES), bf16),
            dma((CHUNKS, group)), dma((CHUNKS, group)),
            dma((n_col,)), dma((n_col,)),
            dma((n_col,)), dma((n_col,)),
            dma((n_col,)), dma((n_col,)),
            dma((CHUNKS, n_col)), dma((CHUNKS, n_col)),
            dma((n_col,)), dma((n_col,)),
            dma((4,)),
        ],
        compiler_params=pltpu.CompilerParams(
            collective_id=0, has_side_effects=True, vmem_limit_bytes=62 * 1024 * 1024
        ),
    )(activations, w, tile_ids.reshape(cap), tile_counts.reshape(1), upstream)
    return (output, grad.reshape(1, 1, cap, TILE * TILE))


def solution(mesh):
    return jax.shard_map(
        body,
        mesh=mesh,
        in_specs=(
            P("col", "row"),
            P("col", "row", None, None),
            P("col", "row", None),
            P("col", "row"),
            P("col", "row"),
        ),
        out_specs=(P("col", "row"), P("col", "row", None, None)),
        check_vma=False,
    )
```

```python
import functools

import jax
import jax.numpy as jnp
from jax import lax
from jax.experimental import pallas as pl
from jax.experimental.pallas import tpu as pltpu
from jax.sharding import PartitionSpec as P

TILE = 64
LANES = 128
CHUNKS = 4
UNROLL = 3
MESH = pl.DeviceIdType.MESH


def gelu_parts(pre):
    cumul = 0.5 * (1.0 + lax.erf(pre * 0.7071067811865476))
    density = jnp.exp(-0.5 * pre * pre) * 0.3989422804014327
    return (cumul, density)


def kernel(
    n_row, n_col, per_col,
    x_hbm, w_ref, ids_ref, cnt_ref, up_hbm, out_ref, grad_ref, *scratch,
):
    xg, scratch = scratch[:CHUNKS], scratch[CHUNKS:]
    (
        x_ref, up_ref, natural, mixed, wsrc, sendx, recvx, wbuf, wpl, xall, idsrc, idq, idc, sidq, sidc, table, stable,
        prod, run, g, gt, dsend, drecv,
        xg_s, xg_r, ic_s, ic_r, iq_s, iq_r, w_s, w_r, xz_s, xz_r, d_s, d_r, loc,
    ) = scratch
    cap = ids_ref.shape[0]
    half = cap // 2
    slots = n_col * cap
    group = n_row // n_col
    line = n_col
    chunks = len(xg)
    all_tiles, packed_rows, _ = xg[0].shape
    tc = 2 * packed_rows
    own_tiles = all_tiles // group
    n_pair = g.shape[0]
    col = lax.axis_index("col")
    row = lax.axis_index("row")
    z = row // group
    x = lax.rem(row, group)

    def member(k):
        return lax.rem(x + k, group)

    def at_line(k):
        return lax.rem(z + k, line)

    def at_col(k):
        return lax.rem(col + k, n_col)

    copy_x = pltpu.make_async_copy(x_hbm, x_ref, loc.at[2])
    copy_up = pltpu.make_async_copy(up_hbm, up_ref, loc.at[3])
    copy_x.start()
    copy_up.start()
    barrier = pltpu.get_barrier_semaphore()
    for k in range(1, group):
        pl.semaphore_signal(barrier, inc=1, device_id={"row": z * group + member(k)}, device_id_type=MESH)
    for k in range(1, line):
        pl.semaphore_signal(barrier, inc=1, device_id={"row": at_line(k) * group + x}, device_id_type=MESH)
    for k in range(1, n_col):
        pl.semaphore_signal(barrier, inc=1, device_id={"col": at_col(k)}, device_id_type=MESH)

    lane8 = lax.broadcasted_iota(jnp.int32, (8, LANES), 1)
    row8 = lax.broadcasted_iota(jnp.int32, (8, LANES), 0)
    ids = jnp.zeros((8, LANES), jnp.int32)
    for s in range(cap):
        ids = jnp.where(lane8 == s, ids_ref[s], ids)
    feature = ids // per_col
    hidden_tile = ids - feature * per_col
    packed = jnp.where(row8 == 0, feature, jnp.where(row8 == 1, hidden_tile, lax.rem(hidden_tile, 2)))
    packed = jnp.where(lane8 == cap, cnt_ref[0], packed)
    idsrc[...] = packed
    idc[col] = packed

    def pack(c):
        for t in range(own_tiles):
            lanes = slice(t * TILE, (t + 1) * TILE)
            top = x_ref[c * tc : c * tc + packed_rows, lanes].astype(jnp.float32)
            bottom = x_ref[c * tc + packed_rows : (c + 1) * tc, lanes].astype(jnp.float32)
            xg[c][x * own_tiles + t] = jnp.concatenate([top, bottom], axis=1).astype(jnp.bfloat16)

    copy_x.wait()
    pack(0)
    pl.semaphore_wait(barrier, group + line + n_col - 3)

    def remote(src, dst, send, recv, target):
        return pltpu.make_async_remote_copy(
            src_ref=src, dst_ref=dst, send_sem=send, recv_sem=recv, device_id=target, device_id_type=MESH
        )

    def ids_col(k, owner):
        return remote(idsrc, idc.at[owner], ic_s.at[k], ic_r.at[owner], {"col": at_col(k)})

    def ids_line(k, owner):
        to = at_line(k)
        return remote(idc.at[to], idq.at[owner], iq_s.at[k], iq_r.at[owner], {"row": to * group + x})

    def w_col(k, owner):
        return remote(wsrc, wbuf.at[owner], w_s.at[k], w_r.at[owner], {"col": at_col(k)})

    def x_group(c, k, owner):
        mine = xg[c].at[pl.ds(x * own_tiles, own_tiles)]
        theirs = xg[c].at[pl.ds(owner * own_tiles, own_tiles)]
        return remote(mine, theirs, xg_s.at[c, k], xg_r.at[c, owner], {"row": z * group + member(k)})

    def x_line(c, k, owner):
        to = at_line(k)
        return remote(
            sendx.at[c, to], recvx.at[c, owner], xz_s.at[c, k], xz_r.at[c, owner], {"row": to * group + x}
        )

    def d_col(k, owner):
        to = at_col(k)
        return remote(dsend.at[to], drecv.at[owner], d_s.at[k], d_r.at[owner], {"col": to})

    for k in range(1, n_col):
        ids_col(k, col).start()
    for k in range(1, group):
        x_group(0, k, x).start()
    for c in range(1, chunks):
        pack(c)
        for k in range(1, group):
            x_group(c, k, x).start()

    for k in range(1, n_col):
        ids_col(k, at_col(k)).wait_recv()
    for k in range(1, line):
        ids_line(k, z).start()
    idq[z] = idc[z]
    copy_c = pltpu.make_async_copy(idc, sidc, loc.at[1])
    copy_c.start()

    lane_half = lax.broadcasted_iota(jnp.int32, (TILE, LANES), 1) // TILE
    low = lax.broadcasted_iota(jnp.int32, (TILE // 2, LANES), 1) < TILE
    even, odd = pl.ds(0, TILE // 2, stride=2), pl.ds(1, TILE // 2, stride=2)
    for j in range(TILE // 2):
        natural[:, j, :] = w_ref[:, j * LANES : (j + 1) * LANES].astype(jnp.float32)
    for j in range(half):
        one, two = natural[j], natural[j + half]
        mixed[even, :] = jnp.where(low, one, pltpu.roll(two, TILE, 1))
        mixed[odd, :] = jnp.where(low, pltpu.roll(one, TILE, 1), two)
        wsrc[j] = mixed[...].astype(jnp.bfloat16)
    wbuf[col] = wsrc[...]
    for k in range(1, n_col):
        w_col(k, col).start()

    for k in range(1, line):
        ids_line(k, at_line(k)).wait_recv()
    copy_q = pltpu.make_async_copy(idq, sidq, loc.at[0])
    copy_q.start()
    copy_c.wait()
    copy_q.wait()

    for c in range(chunks):
        for k in range(1, group):
            x_group(c, k, member(k)).wait_recv()
        for k in range(line - 1, 0, -1):
            to = at_line(k)
            for s in range(cap):
                sendx[c, to, s] = xg[c][sidq[to, 0, s]]
            x_line(c, k, z).start()
        for s in range(cap):
            recvx[c, z, s] = xg[c][sidq[z, 0, s]]

    width = table.shape[1]
    lanes_s = lax.broadcasted_iota(jnp.int32, (slots, width), 1)
    rows_s = lax.broadcasted_iota(jnp.int32, (slots, width), 0)
    key_row = jnp.full((1, width), per_col + 1, jnp.int32) * slots + slots
    key_col = jnp.zeros((slots, width), jnp.int32)
    lane1 = lax.broadcasted_iota(jnp.int32, (1, width), 1)
    for s in range(slots):
        b, j = s // cap, s % cap
        f = jnp.where(j < sidc[b, 0, cap], sidc[b, 1, j], per_col)
        key_row = jnp.where(lane1 == s, f * slots + s, key_row)
        key_col = jnp.where(rows_s == s, f, key_col)
    ahead = jnp.where(key_row < key_col * slots + rows_s, 1, 0)
    rank = jnp.sum(ahead, axis=1, keepdims=True)
    here = jnp.where(rank == lanes_s, 1, 0)
    table[0:1, :] = jnp.sum(here * rows_s, axis=0, keepdims=True)
    table[1:2, :] = jnp.sum(here * key_col, axis=0, keepdims=True)
    upto = jnp.sum(jnp.where(key_col <= lanes_s, 1, 0), axis=0, keepdims=True)
    some = jnp.sum(jnp.where(key_col == lanes_s, 1, 0), axis=0, keepdims=True)
    table[2:3, :] = jnp.where(some > 0, upto - 1, slots)
    table[3:8, :] = jnp.zeros((5, width), jnp.int32)
    copy_t = pltpu.make_async_copy(table, stable, loc.at[0])
    copy_t.start()
    copy_t.wait()

    for k in range(1, n_col):
        w_col(k, at_col(k)).wait_recv()

    def place_weights(b, carry):
        for s in range(cap):
            side = sidc[b, 2, s]
            both = jnp.where(lane_half == s // half, wbuf[b, s % half].astype(jnp.float32), 0.0)
            both = both + pltpu.roll(both, TILE, 1)
            placed = jnp.where(lane_half == side, both, 0.0).astype(jnp.bfloat16)
            wpl[b * cap + s, :TILE] = placed
            wpl[b * cap + s, TILE:] = placed
        return carry

    lax.fori_loop(0, n_col, place_weights, 0)
    run[slots] = jnp.zeros((tc, LANES), jnp.float32)

    packed_half = lax.broadcasted_iota(jnp.int32, (packed_rows, LANES), 1) // TILE
    first = jnp.where(packed_half == 0, 1.0, 0.0).astype(jnp.bfloat16)
    second = jnp.where(packed_half == 1, 1.0, 0.0).astype(jnp.bfloat16)

    def chunk_rows(c):
        return pl.ds(pl.multiple_of(c * tc, tc), tc)

    def products(c, b):
        for s in range(cap):
            tile = recvx[c, b, s]
            spread = jnp.concatenate([tile * first, tile * second], axis=0)
            xall[b * cap + s, chunk_rows(c)] = spread
            prod[b * cap + s] = jnp.dot(spread, wpl[b * cap + s], preferred_element_type=jnp.float32)

    def hidden(c, last):
        products(c, z)

        def later(k, carry):
            b = at_line(k)
            x_line(c, k, b).wait_recv()
            products(c, b)
            return carry

        lax.fori_loop(1, line, later, 0)

        def add_run(r, held):
            same = jnp.where(stable[1, r] == stable[1, jnp.maximum(r - 1, 0)], 1.0, 0.0)
            total = prod[stable[0, r]] + held * same
            run[r] = total
            return total

        lax.fori_loop(0, slots, add_run, jnp.zeros((tc, LANES), jnp.float32), unroll=4)

        rows = chunk_rows(c)

        def gelu_pair(p, carry):
            lanes = pl.ds(pl.multiple_of(p * LANES, LANES), LANES)
            v = run[stable[2, 2 * p]] + run[stable[2, 2 * p + 1]]
            cumul, density = gelu_parts(v)
            out_ref[rows, lanes] = (v * cumul).astype(jnp.bfloat16)
            g[p, rows] = (up_ref[rows, lanes].astype(jnp.float32) * (cumul + v * density)).astype(jnp.bfloat16)
            if last:
                both = g[p].astype(jnp.float32).T.astype(jnp.bfloat16)
                gt[2 * p] = both[:TILE]
                gt[2 * p + 1] = both[TILE:]
            return carry

        lax.fori_loop(0, n_pair, gelu_pair, 0, unroll=UNROLL)

    def terms(b):
        for j in range(half):
            parts = []
            for i in (j, j + half):
                parts.append(jnp.dot(gt[sidc[b, 1, i]], xall[b * cap + i], preferred_element_type=jnp.float32))
            turned = jnp.concatenate(parts, axis=0).T
            dsend[b, j] = (turned[:TILE] + turned[TILE:]).astype(jnp.bfloat16)

    copy_up.wait()

    def early(c, carry):
        hidden(c, False)
        return carry

    lax.fori_loop(0, chunks - 1, early, 0)
    hidden(chunks - 1, True)

    def send_terms(i, carry):
        k = 1 + lax.rem(n_col // 2 - 1 + i, n_col - 1)
        terms(at_col(k))
        d_col(k, col).start()
        return carry

    lax.fori_loop(0, n_col - 1, send_terms, 0)
    terms(col)
    for k in range(1, n_col):
        d_col(k, at_col(k)).wait_recv()
    own_count = cnt_ref[0]
    for j in range(half):
        total = dsend[col, j].astype(jnp.float32)
        for k in range(1, n_col):
            total = total + drecv[at_col(k), j].astype(jnp.float32)
        mixed[...] = jnp.where(lane_half * half + j < own_count, total, 0.0)
        one, two = mixed[even, :], mixed[odd, :]
        natural[j] = jnp.where(low, one, pltpu.roll(two, TILE, 1))
        natural[j + half] = jnp.where(low, pltpu.roll(one, TILE, 1), two)
    for j in range(TILE // 2):
        grad_ref[:, j * LANES : (j + 1) * LANES] = natural[:, j, :].astype(jnp.bfloat16)

    for c in range(chunks):
        for k in range(1, group):
            x_group(c, k, x).wait_send()
        for k in range(1, line):
            x_line(c, k, z).wait_send()
    for k in range(1, line):
        ids_line(k, z).wait_send()
    for k in range(1, n_col):
        ids_col(k, col).wait_send()
        w_col(k, col).wait_send()
        d_col(k, col).wait_send()


def body(activations, weight_tiles, tile_ids, tile_counts, upstream):
    n_row, n_col = lax.axis_size("row"), lax.axis_size("col")
    group = n_row // n_col
    tok, own_width = activations.shape
    ff_local = upstream.shape[1]
    per_col = ff_local // TILE
    cap = weight_tiles.shape[2]
    half = cap // 2
    slots = n_col * cap
    own_tiles = own_width // TILE
    tc = tok // CHUNKS
    rows = tc // 2
    width = -(-max(slots, per_col) // LANES) * LANES
    w = weight_tiles.reshape(cap, TILE * TILE)
    bf16, f32, i32 = jnp.bfloat16, jnp.float32, jnp.int32
    vmem = pl.BlockSpec(memory_space=pltpu.VMEM)
    smem = pl.BlockSpec(memory_space=pltpu.SMEM)
    hbm = pl.BlockSpec(memory_space=pltpu.HBM)
    dma = pltpu.SemaphoreType.DMA
    n_pair = ff_local // LANES
    output, grad = pl.pallas_call(
        functools.partial(kernel, n_row, n_col, per_col),
        out_shape=(
            jax.ShapeDtypeStruct((tok, ff_local), bf16),
            jax.ShapeDtypeStruct((cap, TILE * TILE), bf16),
        ),
        in_specs=[hbm, vmem, smem, smem, hbm],
        out_specs=(vmem, vmem),
        scratch_shapes=[
            *[pltpu.VMEM((group * own_tiles, rows, LANES), bf16) for _ in range(CHUNKS)],
            pltpu.VMEM(activations.shape, bf16),
            pltpu.VMEM(upstream.shape, bf16),
            pltpu.VMEM((cap, TILE // 2, LANES), f32),
            pltpu.VMEM((TILE, LANES), f32),
            pltpu.VMEM((half, TILE, LANES), bf16),
            pltpu.VMEM((CHUNKS, n_col, cap, rows, LANES), bf16),
            pltpu.VMEM((CHUNKS, n_col, cap, rows, LANES), bf16),
            pltpu.VMEM((n_col, half, TILE, LANES), bf16),
            pltpu.VMEM((slots, 2 * TILE, LANES), bf16),
            pltpu.VMEM((slots, tok, LANES), bf16),
            pltpu.VMEM((8, LANES), i32),
            pltpu.VMEM((n_col, 8, LANES), i32),
            pltpu.VMEM((n_col, 8, LANES), i32),
            pltpu.SMEM((n_col, 8, LANES), i32),
            pltpu.SMEM((n_col, 8, LANES), i32),
            pltpu.VMEM((8, width), i32),
            pltpu.SMEM((8, width), i32),
            pltpu.VMEM((slots, tc, LANES), f32),
            pltpu.VMEM((slots + 1, tc, LANES), f32),
            pltpu.VMEM((n_pair, tok, LANES), bf16),
            pltpu.VMEM((per_col, TILE, tok), bf16),
            pltpu.VMEM((n_col, half, TILE, LANES), bf16),
            pltpu.VMEM((n_col, half, TILE, LANES), bf16),
            dma((CHUNKS, group)), dma((CHUNKS, group)),
            dma((n_col,)), dma((n_col,)),
            dma((n_col,)), dma((n_col,)),
            dma((n_col,)), dma((n_col,)),
            dma((CHUNKS, n_col)), dma((CHUNKS, n_col)),
            dma((n_col,)), dma((n_col,)),
            dma((4,)),
        ],
        compiler_params=pltpu.CompilerParams(
            collective_id=0, has_side_effects=True, vmem_limit_bytes=52 * 1024 * 1024
        ),
    )(activations, w, tile_ids.reshape(cap), tile_counts.reshape(1), upstream)
    return (output, grad.reshape(1, 1, cap, TILE * TILE))


def solution(mesh):
    return jax.shard_map(
        body,
        mesh=mesh,
        in_specs=(
            P("col", "row"),
            P("col", "row", None, None),
            P("col", "row", None),
            P("col", "row"),
            P("col", "row"),
        ),
        out_specs=(P("col", "row"), P("col", "row", None, None)),
        check_vma=False,
    )
```

```python
import functools

import jax
import jax.numpy as jnp
from jax import lax
from jax.experimental import pallas as pl
from jax.experimental.pallas import tpu as pltpu
from jax.sharding import PartitionSpec as P

TILE = 64
LANES = 128
CHUNKS = 4
UNROLL = 3
MESH = pl.DeviceIdType.MESH


def gelu_parts(pre):
    cumul = 0.5 * (1.0 + lax.erf(pre * 0.7071067811865476))
    density = jnp.exp(-0.5 * pre * pre) * 0.3989422804014327
    return (cumul, density)


def kernel(
    n_row, n_col, per_col,
    x_hbm, w_hbm, ids_ref, cnt_ref, up_hbm, out_ref, grad_ref, *scratch,
):
    xg, scratch = scratch[:CHUNKS], scratch[CHUNKS:]
    (
        x_ref, up_ref, w_ref, natural, mixed, wsrc, sendx, recvx, wbuf, wpl, xall, idsrc, idq, idc, sidq, sidc, table, stable,
        prod, run, g, gt, dsend, drecv,
        xg_s, xg_r, ic_s, ic_r, iq_s, iq_r, w_s, w_r, xz_s, xz_r, d_s, d_r, loc,
    ) = scratch
    cap = ids_ref.shape[0]
    half = cap // 2
    slots = n_col * cap
    group = n_row // n_col
    line = n_col
    chunks = len(xg)
    all_tiles, packed_rows, _ = xg[0].shape
    tc = 2 * packed_rows
    own_tiles = all_tiles // group
    n_pair = g.shape[0]
    col = lax.axis_index("col")
    row = lax.axis_index("row")
    z = row // group
    x = lax.rem(row, group)

    def member(k):
        return lax.rem(x + k, group)

    def at_line(k):
        return lax.rem(z + k, line)

    def at_col(k):
        return lax.rem(col + k, n_col)

    copy_x = pltpu.make_async_copy(x_hbm, x_ref, loc.at[2])
    copy_up = pltpu.make_async_copy(up_hbm, up_ref, loc.at[3])
    copy_x.start()
    copy_w = pltpu.make_async_copy(w_hbm, w_ref, loc.at[4])
    copy_w.start()
    copy_up.start()
    barrier = pltpu.get_barrier_semaphore()
    for k in range(1, group):
        pl.semaphore_signal(barrier, inc=1, device_id={"row": z * group + member(k)}, device_id_type=MESH)
    for k in range(1, line):
        pl.semaphore_signal(barrier, inc=1, device_id={"row": at_line(k) * group + x}, device_id_type=MESH)
    for k in range(1, n_col):
        pl.semaphore_signal(barrier, inc=1, device_id={"col": at_col(k)}, device_id_type=MESH)

    lane8 = lax.broadcasted_iota(jnp.int32, (8, LANES), 1)
    row8 = lax.broadcasted_iota(jnp.int32, (8, LANES), 0)
    ids = jnp.zeros((8, LANES), jnp.int32)
    for s in range(cap):
        ids = jnp.where(lane8 == s, ids_ref[s], ids)
    feature = ids // per_col
    hidden_tile = ids - feature * per_col
    packed = jnp.where(row8 == 0, feature, jnp.where(row8 == 1, hidden_tile, lax.rem(hidden_tile, 2)))
    packed = jnp.where(lane8 == cap, cnt_ref[0], packed)
    idsrc[...] = packed
    idc[col] = packed

    def pack(c):
        for t in range(own_tiles):
            lanes = slice(t * TILE, (t + 1) * TILE)
            top = x_ref[c * tc : c * tc + packed_rows, lanes].astype(jnp.float32)
            bottom = x_ref[c * tc + packed_rows : (c + 1) * tc, lanes].astype(jnp.float32)
            xg[c][x * own_tiles + t] = jnp.concatenate([top, bottom], axis=1).astype(jnp.bfloat16)

    copy_x.wait()
    pack(0)
    pl.semaphore_wait(barrier, group + line + n_col - 3)

    def remote(src, dst, send, recv, target):
        return pltpu.make_async_remote_copy(
            src_ref=src, dst_ref=dst, send_sem=send, recv_sem=recv, device_id=target, device_id_type=MESH
        )

    def ids_col(k, owner):
        return remote(idsrc, idc.at[owner], ic_s.at[k], ic_r.at[owner], {"col": at_col(k)})

    def ids_line(k, owner):
        to = at_line(k)
        return remote(idc.at[to], idq.at[owner], iq_s.at[k], iq_r.at[owner], {"row": to * group + x})

    def w_col(k, owner):
        return remote(wsrc, wbuf.at[owner], w_s.at[k], w_r.at[owner], {"col": at_col(k)})

    def x_group(c, k, owner):
        mine = xg[c].at[pl.ds(x * own_tiles, own_tiles)]
        theirs = xg[c].at[pl.ds(owner * own_tiles, own_tiles)]
        return remote(mine, theirs, xg_s.at[c, k], xg_r.at[c, owner], {"row": z * group + member(k)})

    def x_line(c, k, owner):
        to = at_line(k)
        return remote(
            sendx.at[c, to], recvx.at[c, owner], xz_s.at[c, k], xz_r.at[c, owner], {"row": to * group + x}
        )

    def d_col(k, owner):
        to = at_col(k)
        return remote(dsend.at[to], drecv.at[owner], d_s.at[k], d_r.at[owner], {"col": to})

    for k in range(1, n_col):
        ids_col(k, col).start()
    for k in range(1, group):
        x_group(0, k, x).start()

    def swap(c):
        pack(c)
        for k in range(1, group):
            x_group(c, k, x).start()

    if chunks > 1:
        swap(1)
    for k in range(1, n_col):
        ids_col(k, at_col(k)).wait_recv()
    for k in range(1, line):
        ids_line(k, z).start()
    idq[z] = idc[z]
    copy_c = pltpu.make_async_copy(idc, sidc, loc.at[1])
    copy_c.start()

    for c in range(2, chunks):
        swap(c)
    for k in range(1, line):
        ids_line(k, at_line(k)).wait_recv()
    copy_q = pltpu.make_async_copy(idq, sidq, loc.at[0])
    copy_q.start()
    copy_c.wait()
    copy_q.wait()

    def send_chunk(c):
        for k in range(1, group):
            x_group(c, k, member(k)).wait_recv()
        for k in range(line - 1, 0, -1):
            to = at_line(k)
            for s in range(cap):
                sendx[c, to, s] = xg[c][sidq[to, 0, s]]
            x_line(c, k, z).start()
        for s in range(cap):
            recvx[c, z, s] = xg[c][sidq[z, 0, s]]

    send_chunk(0)

    lane_half = lax.broadcasted_iota(jnp.int32, (TILE, LANES), 1) // TILE
    low = lax.broadcasted_iota(jnp.int32, (TILE // 2, LANES), 1) < TILE
    even, odd = pl.ds(0, TILE // 2, stride=2), pl.ds(1, TILE // 2, stride=2)
    copy_w.wait()
    for j in range(TILE // 2):
        natural[:, j, :] = w_ref[:, j * LANES : (j + 1) * LANES].astype(jnp.float32)
    for j in range(half):
        one, two = natural[j], natural[j + half]
        mixed[even, :] = jnp.where(low, one, pltpu.roll(two, TILE, 1))
        mixed[odd, :] = jnp.where(low, pltpu.roll(one, TILE, 1), two)
        wsrc[j] = mixed[...].astype(jnp.bfloat16)
    wbuf[col] = wsrc[...]
    for k in range(1, n_col):
        w_col(k, col).start()

    for c in range(1, chunks):
        send_chunk(c)

    width = table.shape[1]
    lanes_s = lax.broadcasted_iota(jnp.int32, (slots, width), 1)
    rows_s = lax.broadcasted_iota(jnp.int32, (slots, width), 0)
    key_row = jnp.full((1, width), per_col + 1, jnp.int32) * slots + slots
    key_col = jnp.zeros((slots, width), jnp.int32)
    lane1 = lax.broadcasted_iota(jnp.int32, (1, width), 1)
    for s in range(slots):
        b, j = s // cap, s % cap
        f = jnp.where(j < sidc[b, 0, cap], sidc[b, 1, j], per_col)
        key_row = jnp.where(lane1 == s, f * slots + s, key_row)
        key_col = jnp.where(rows_s == s, f, key_col)
    ahead = jnp.where(key_row < key_col * slots + rows_s, 1, 0)
    rank = jnp.sum(ahead, axis=1, keepdims=True)
    here = jnp.where(rank == lanes_s, 1, 0)
    table[0:1, :] = jnp.sum(here * rows_s, axis=0, keepdims=True)
    table[1:2, :] = jnp.sum(here * key_col, axis=0, keepdims=True)
    upto = jnp.sum(jnp.where(key_col <= lanes_s, 1, 0), axis=0, keepdims=True)
    some = jnp.sum(jnp.where(key_col == lanes_s, 1, 0), axis=0, keepdims=True)
    table[2:3, :] = jnp.where(some > 0, upto - 1, slots)
    table[3:8, :] = jnp.zeros((5, width), jnp.int32)
    copy_t = pltpu.make_async_copy(table, stable, loc.at[0])
    copy_t.start()
    copy_t.wait()

    for k in range(1, n_col):
        w_col(k, at_col(k)).wait_recv()

    def place_weights(b, carry):
        for s in range(cap):
            side = sidc[b, 2, s]
            both = jnp.where(lane_half == s // half, wbuf[b, s % half].astype(jnp.float32), 0.0)
            both = both + pltpu.roll(both, TILE, 1)
            placed = jnp.where(lane_half == side, both, 0.0).astype(jnp.bfloat16)
            wpl[b * cap + s, :TILE] = placed
            wpl[b * cap + s, TILE:] = placed
        return carry

    lax.fori_loop(0, n_col, place_weights, 0)
    run[slots] = jnp.zeros((tc, LANES), jnp.float32)

    packed_half = lax.broadcasted_iota(jnp.int32, (packed_rows, LANES), 1) // TILE
    first = jnp.where(packed_half == 0, 1.0, 0.0).astype(jnp.bfloat16)
    second = jnp.where(packed_half == 1, 1.0, 0.0).astype(jnp.bfloat16)

    def chunk_rows(c):
        return pl.ds(pl.multiple_of(c * tc, tc), tc)

    def products(c, b):
        for s in range(cap):
            tile = recvx[c, b, s]
            spread = jnp.concatenate([tile * first, tile * second], axis=0)
            xall[b * cap + s, chunk_rows(c)] = spread
            prod[b * cap + s] = jnp.dot(spread, wpl[b * cap + s], preferred_element_type=jnp.float32)

    def hidden(c, last):
        products(c, z)

        def later(k, carry):
            b = at_line(k)
            x_line(c, k, b).wait_recv()
            products(c, b)
            return carry

        lax.fori_loop(1, line, later, 0)

        def add_run(r, held):
            same = jnp.where(stable[1, r] == stable[1, jnp.maximum(r - 1, 0)], 1.0, 0.0)
            total = prod[stable[0, r]] + held * same
            run[r] = total
            return total

        lax.fori_loop(0, slots, add_run, jnp.zeros((tc, LANES), jnp.float32), unroll=4)

        rows = chunk_rows(c)

        def gelu_pair(p, carry):
            lanes = pl.ds(pl.multiple_of(p * LANES, LANES), LANES)
            v = run[stable[2, 2 * p]] + run[stable[2, 2 * p + 1]]
            cumul, density = gelu_parts(v)
            out_ref[rows, lanes] = (v * cumul).astype(jnp.bfloat16)
            g[p, rows] = (up_ref[rows, lanes].astype(jnp.float32) * (cumul + v * density)).astype(jnp.bfloat16)
            if last:
                both = g[p].astype(jnp.float32).T.astype(jnp.bfloat16)
                gt[2 * p] = both[:TILE]
                gt[2 * p + 1] = both[TILE:]
            return carry

        lax.fori_loop(0, n_pair, gelu_pair, 0, unroll=UNROLL)

    def terms(b):
        for j in range(half):
            parts = []
            for i in (j, j + half):
                parts.append(jnp.dot(gt[sidc[b, 1, i]], xall[b * cap + i], preferred_element_type=jnp.float32))
            turned = jnp.concatenate(parts, axis=0).T
            dsend[b, j] = (turned[:TILE] + turned[TILE:]).astype(jnp.bfloat16)

    copy_up.wait()

    def early(c, carry):
        hidden(c, False)
        return carry

    lax.fori_loop(0, chunks - 1, early, 0)
    hidden(chunks - 1, True)

    odd_core = lax.rem(col, 2)
    mate = 1 + odd_core * (n_col - 2)

    def send_terms(i, carry):
        k = 2 - odd_core + i
        k = k + (i + 1) // (n_col - 1) * (mate - k)
        terms(at_col(k))
        d_col(k, col).start()
        return carry

    lax.fori_loop(0, n_col - 1, send_terms, 0)
    terms(col)
    for k in range(1, n_col):
        d_col(k, at_col(k)).wait_recv()
    own_count = cnt_ref[0]
    for j in range(half):
        total = dsend[col, j].astype(jnp.float32)
        for k in range(1, n_col):
            total = total + drecv[at_col(k), j].astype(jnp.float32)
        mixed[...] = jnp.where(lane_half * half + j < own_count, total, 0.0)
        one, two = mixed[even, :], mixed[odd, :]
        natural[j] = jnp.where(low, one, pltpu.roll(two, TILE, 1))
        natural[j + half] = jnp.where(low, pltpu.roll(one, TILE, 1), two)
    for j in range(TILE // 2):
        grad_ref[:, j * LANES : (j + 1) * LANES] = natural[:, j, :].astype(jnp.bfloat16)

    for c in range(chunks):
        for k in range(1, group):
            x_group(c, k, x).wait_send()
        for k in range(1, line):
            x_line(c, k, z).wait_send()
    for k in range(1, line):
        ids_line(k, z).wait_send()
    for k in range(1, n_col):
        ids_col(k, col).wait_send()
        w_col(k, col).wait_send()
        d_col(k, col).wait_send()


def body(activations, weight_tiles, tile_ids, tile_counts, upstream):
    n_row, n_col = lax.axis_size("row"), lax.axis_size("col")
    group = n_row // n_col
    tok, own_width = activations.shape
    ff_local = upstream.shape[1]
    per_col = ff_local // TILE
    cap = weight_tiles.shape[2]
    half = cap // 2
    slots = n_col * cap
    own_tiles = own_width // TILE
    tc = tok // CHUNKS
    rows = tc // 2
    width = -(-max(slots, per_col) // LANES) * LANES
    w = weight_tiles.reshape(cap, TILE * TILE)
    bf16, f32, i32 = jnp.bfloat16, jnp.float32, jnp.int32
    vmem = pl.BlockSpec(memory_space=pltpu.VMEM)
    smem = pl.BlockSpec(memory_space=pltpu.SMEM)
    hbm = pl.BlockSpec(memory_space=pltpu.HBM)
    dma = pltpu.SemaphoreType.DMA
    in_hbm = functools.partial(pltpu.with_memory_space_constraint, memory_space=pltpu.HBM)
    n_pair = ff_local // LANES
    output, grad = pl.pallas_call(
        functools.partial(kernel, n_row, n_col, per_col),
        out_shape=(
            jax.ShapeDtypeStruct((tok, ff_local), bf16),
            jax.ShapeDtypeStruct((cap, TILE * TILE), bf16),
        ),
        in_specs=[hbm, hbm, smem, smem, hbm],
        out_specs=(vmem, vmem),
        scratch_shapes=[
            *[pltpu.VMEM((group * own_tiles, rows, LANES), bf16) for _ in range(CHUNKS)],
            pltpu.VMEM(activations.shape, bf16),
            pltpu.VMEM(upstream.shape, bf16),
            pltpu.VMEM(w.shape, bf16),
            pltpu.VMEM((cap, TILE // 2, LANES), f32),
            pltpu.VMEM((TILE, LANES), f32),
            pltpu.VMEM((half, TILE, LANES), bf16),
            pltpu.VMEM((CHUNKS, n_col, cap, rows, LANES), bf16),
            pltpu.VMEM((CHUNKS, n_col, cap, rows, LANES), bf16),
            pltpu.VMEM((n_col, half, TILE, LANES), bf16),
            pltpu.VMEM((slots, 2 * TILE, LANES), bf16),
            pltpu.VMEM((slots, tok, LANES), bf16),
            pltpu.VMEM((8, LANES), i32),
            pltpu.VMEM((n_col, 8, LANES), i32),
            pltpu.VMEM((n_col, 8, LANES), i32),
            pltpu.SMEM((n_col, 8, LANES), i32),
            pltpu.SMEM((n_col, 8, LANES), i32),
            pltpu.VMEM((8, width), i32),
            pltpu.SMEM((8, width), i32),
            pltpu.VMEM((slots, tc, LANES), f32),
            pltpu.VMEM((slots + 1, tc, LANES), f32),
            pltpu.VMEM((n_pair, tok, LANES), bf16),
            pltpu.VMEM((per_col, TILE, tok), bf16),
            pltpu.VMEM((n_col, half, TILE, LANES), bf16),
            pltpu.VMEM((n_col, half, TILE, LANES), bf16),
            dma((CHUNKS, group)), dma((CHUNKS, group)),
            dma((n_col,)), dma((n_col,)),
            dma((n_col,)), dma((n_col,)),
            dma((n_col,)), dma((n_col,)),
            dma((CHUNKS, n_col)), dma((CHUNKS, n_col)),
            dma((n_col,)), dma((n_col,)),
            dma((5,)),
        ],
        compiler_params=pltpu.CompilerParams(
            collective_id=0, has_side_effects=True, vmem_limit_bytes=48 * 1024 * 1024
        ),
    )(in_hbm(activations), in_hbm(w), tile_ids.reshape(cap), tile_counts.reshape(1), in_hbm(upstream))
    return (output, grad.reshape(1, 1, cap, TILE * TILE))


def solution(mesh):
    return jax.shard_map(
        body,
        mesh=mesh,
        in_specs=(
            P("col", "row"),
            P("col", "row", None, None),
            P("col", "row", None),
            P("col", "row"),
            P("col", "row"),
        ),
        out_specs=(P("col", "row"), P("col", "row", None, None)),
        check_vma=False,
    )
```

```python
import functools

import jax
import jax.numpy as jnp
from jax import lax
from jax.experimental import pallas as pl
from jax.experimental.pallas import tpu as pltpu
from jax.sharding import PartitionSpec as P

TILE = 64
LANES = 128
CHUNKS = 4
UNROLL = 4
MESH = pl.DeviceIdType.MESH


def gelu_parts(pre):
    cumul = 0.5 * (1.0 + lax.erf(pre * 0.7071067811865476))
    density = jnp.exp(-0.5 * pre * pre) * 0.3989422804014327
    return (cumul, density)


def kernel(
    n_row, n_col, per_col,
    x_hbm, w_hbm, ids_hbm, cnt_ref, up_hbm, out_ref, grad_ref, *scratch,
):
    xg, scratch = scratch[:CHUNKS], scratch[CHUNKS:]
    (
        ids_ref, x_ref, up_ref, w_ref, natural, mixed, wsrc, sendx, recvx, wbuf, wpl, xall, idsrc, idq, idc, sidq, sidc, table, stable,
        prod, run, g, gt, dsend, drecv,
        xg_s, xg_r, ic_s, ic_r, iq_s, iq_r, w_s, w_r, xz_s, xz_r, d_s, d_r, loc,
    ) = scratch
    cap = ids_hbm.shape[0]
    half = cap // 2
    slots = n_col * cap
    group = n_row // n_col
    line = n_col
    chunks = len(xg)
    all_tiles, packed_rows, _ = xg[0].shape
    tc = 2 * packed_rows
    own_tiles = all_tiles // group
    n_pair = g.shape[0]
    col = lax.axis_index("col")
    row = lax.axis_index("row")
    z = row // group
    x = lax.rem(row, group)

    def member(k):
        return lax.rem(x + k, group)

    def at_line(k):
        return lax.rem(z + k, line)

    def at_col(k):
        return lax.rem(col + k, n_col)

    copy_ids = pltpu.make_async_copy(ids_hbm, ids_ref, loc.at[0])
    copy_x = [
        pltpu.make_async_copy(x_hbm.at[pl.ds(c * tc, tc)], x_ref.at[pl.ds(c * tc, tc)], loc.at[5 + c])
        for c in range(chunks)
    ]
    copy_up = pltpu.make_async_copy(up_hbm, up_ref, loc.at[3])
    copy_ids.start()
    for copy in copy_x:
        copy.start()
    copy_w = pltpu.make_async_copy(w_hbm, w_ref, loc.at[4])
    copy_w.start()
    copy_up.start()
    barrier = pltpu.get_barrier_semaphore()
    for k in range(1, group):
        pl.semaphore_signal(barrier, inc=1, device_id={"row": z * group + member(k)}, device_id_type=MESH)
    for k in range(1, line):
        pl.semaphore_signal(barrier, inc=1, device_id={"row": at_line(k) * group + x}, device_id_type=MESH)
    for k in range(1, n_col):
        pl.semaphore_signal(barrier, inc=1, device_id={"col": at_col(k)}, device_id_type=MESH)

    lane8 = lax.broadcasted_iota(jnp.int32, (8, LANES), 1)
    row8 = lax.broadcasted_iota(jnp.int32, (8, LANES), 0)
    ids = jnp.zeros((8, LANES), jnp.int32)
    copy_ids.wait()
    for s in range(cap):
        ids = jnp.where(lane8 == s, ids_ref[s], ids)
    feature = ids // per_col
    hidden_tile = ids - feature * per_col
    packed = jnp.where(row8 == 0, feature, jnp.where(row8 == 1, hidden_tile, lax.rem(hidden_tile, 2)))
    packed = jnp.where(lane8 == cap, cnt_ref[0], packed)
    idsrc[...] = packed
    idc[col] = packed

    def pack(c):
        copy_x[c].wait()
        for t in range(own_tiles):
            lanes = slice(t * TILE, (t + 1) * TILE)
            top = x_ref[c * tc : c * tc + packed_rows, lanes].astype(jnp.float32)
            bottom = x_ref[c * tc + packed_rows : (c + 1) * tc, lanes].astype(jnp.float32)
            xg[c][x * own_tiles + t] = jnp.concatenate([top, bottom], axis=1).astype(jnp.bfloat16)

    pack(0)
    pl.semaphore_wait(barrier, group + line + n_col - 3)

    def remote(src, dst, send, recv, target):
        return pltpu.make_async_remote_copy(
            src_ref=src, dst_ref=dst, send_sem=send, recv_sem=recv, device_id=target, device_id_type=MESH
        )

    def ids_col(k, owner):
        return remote(idsrc, idc.at[owner], ic_s.at[k], ic_r.at[owner], {"col": at_col(k)})

    def ids_line(k, owner):
        to = at_line(k)
        return remote(idc.at[to], idq.at[owner], iq_s.at[k], iq_r.at[owner], {"row": to * group + x})

    def w_col(k, owner):
        return remote(wsrc, wbuf.at[owner], w_s.at[k], w_r.at[owner], {"col": at_col(k)})

    def x_group(c, k, owner):
        mine = xg[c].at[pl.ds(x * own_tiles, own_tiles)]
        theirs = xg[c].at[pl.ds(owner * own_tiles, own_tiles)]
        return remote(mine, theirs, xg_s.at[c, k], xg_r.at[c, owner], {"row": z * group + member(k)})

    def x_line(c, k, owner):
        to = at_line(k)
        return remote(
            sendx.at[c, to], recvx.at[c, owner], xz_s.at[c, k], xz_r.at[c, owner], {"row": to * group + x}
        )

    def d_col(k, owner):
        to = at_col(k)
        return remote(dsend.at[to], drecv.at[owner], d_s.at[k], d_r.at[owner], {"col": to})

    for k in range(1, n_col):
        ids_col(k, col).start()
    for k in range(1, group):
        x_group(0, k, x).start()

    def swap(c):
        pack(c)
        for k in range(1, group):
            x_group(c, k, x).start()

    if chunks > 1:
        swap(1)
    for k in range(1, n_col):
        ids_col(k, at_col(k)).wait_recv()
    for k in range(1, line):
        ids_line(k, z).start()
    idq[z] = idc[z]
    copy_c = pltpu.make_async_copy(idc, sidc, loc.at[1])
    copy_c.start()

    for c in range(2, chunks):
        swap(c)
    for k in range(1, line):
        ids_line(k, at_line(k)).wait_recv()
    copy_q = pltpu.make_async_copy(idq, sidq, loc.at[0])
    copy_q.start()
    copy_c.wait()
    copy_q.wait()

    def send_chunk(c):
        for k in range(1, group):
            x_group(c, k, member(k)).wait_recv()
        for k in range(line - 1, 0, -1):
            to = at_line(k)
            for s in range(cap):
                sendx[c, to, s] = xg[c][sidq[to, 0, s]]
            x_line(c, k, z).start()
        for s in range(cap):
            recvx[c, z, s] = xg[c][sidq[z, 0, s]]

    send_chunk(0)

    lane_half = lax.broadcasted_iota(jnp.int32, (TILE, LANES), 1) // TILE
    low = lax.broadcasted_iota(jnp.int32, (TILE // 2, LANES), 1) < TILE
    even, odd = pl.ds(0, TILE // 2, stride=2), pl.ds(1, TILE // 2, stride=2)
    copy_w.wait()
    for j in range(TILE // 2):
        natural[:, j, :] = w_ref[:, j * LANES : (j + 1) * LANES].astype(jnp.float32)
    for j in range(half):
        one, two = natural[j], natural[j + half]
        mixed[even, :] = jnp.where(low, one, pltpu.roll(two, TILE, 1))
        mixed[odd, :] = jnp.where(low, pltpu.roll(one, TILE, 1), two)
        wsrc[j] = mixed[...].astype(jnp.bfloat16)
    wbuf[col] = wsrc[...]
    for k in range(1, n_col):
        w_col(k, col).start()

    for c in range(1, chunks):
        send_chunk(c)

    width = table.shape[1]
    lanes_s = lax.broadcasted_iota(jnp.int32, (slots, width), 1)
    rows_s = lax.broadcasted_iota(jnp.int32, (slots, width), 0)
    key_row = jnp.full((1, width), per_col + 1, jnp.int32) * slots + slots
    key_col = jnp.zeros((slots, width), jnp.int32)
    lane1 = lax.broadcasted_iota(jnp.int32, (1, width), 1)
    for s in range(slots):
        b, j = s // cap, s % cap
        f = jnp.where(j < sidc[b, 0, cap], sidc[b, 1, j], per_col)
        key_row = jnp.where(lane1 == s, f * slots + s, key_row)
        key_col = jnp.where(rows_s == s, f, key_col)
    ahead = jnp.where(key_row < key_col * slots + rows_s, 1, 0)
    rank = jnp.sum(ahead, axis=1, keepdims=True)
    here = jnp.where(rank == lanes_s, 1, 0)
    table[0:1, :] = jnp.sum(here * rows_s, axis=0, keepdims=True)
    table[1:2, :] = jnp.sum(here * key_col, axis=0, keepdims=True)
    upto = jnp.sum(jnp.where(key_col <= lanes_s, 1, 0), axis=0, keepdims=True)
    some = jnp.sum(jnp.where(key_col == lanes_s, 1, 0), axis=0, keepdims=True)
    table[2:3, :] = jnp.where(some > 0, upto - 1, slots)
    table[3:8, :] = jnp.zeros((5, width), jnp.int32)
    copy_t = pltpu.make_async_copy(table, stable, loc.at[0])
    copy_t.start()
    copy_t.wait()

    for k in range(1, n_col):
        w_col(k, at_col(k)).wait_recv()

    def place_weights(b, carry):
        for s in range(cap):
            side = sidc[b, 2, s]
            both = jnp.where(lane_half == s // half, wbuf[b, s % half].astype(jnp.float32), 0.0)
            both = both + pltpu.roll(both, TILE, 1)
            placed = jnp.where(lane_half == side, both, 0.0).astype(jnp.bfloat16)
            wpl[b * cap + s, :TILE] = placed
            wpl[b * cap + s, TILE:] = placed
        return carry

    lax.fori_loop(0, n_col, place_weights, 0)
    run[slots] = jnp.zeros((tc, LANES), jnp.float32)

    packed_half = lax.broadcasted_iota(jnp.int32, (packed_rows, LANES), 1) // TILE
    first = jnp.where(packed_half == 0, 1.0, 0.0).astype(jnp.bfloat16)
    second = jnp.where(packed_half == 1, 1.0, 0.0).astype(jnp.bfloat16)

    def chunk_rows(c):
        return pl.ds(pl.multiple_of(c * tc, tc), tc)

    def products(c, b):
        for s in range(cap):
            tile = recvx[c, b, s]
            spread = jnp.concatenate([tile * first, tile * second], axis=0)
            xall[b * cap + s, chunk_rows(c)] = spread
            prod[b * cap + s] = jnp.dot(spread, wpl[b * cap + s], preferred_element_type=jnp.float32)

    def hidden(c, last):
        products(c, z)

        def later(k, carry):
            b = at_line(k)
            x_line(c, k, b).wait_recv()
            products(c, b)
            return carry

        lax.fori_loop(1, line, later, 0)

        def add_run(r, held):
            same = jnp.where(stable[1, r] == stable[1, jnp.maximum(r - 1, 0)], 1.0, 0.0)
            total = prod[stable[0, r]] + held * same
            run[r] = total
            return total

        lax.fori_loop(0, slots, add_run, jnp.zeros((tc, LANES), jnp.float32), unroll=8 if slots % 8 == 0 else 1)

        rows = chunk_rows(c)

        def gelu_pair(p, carry):
            lanes = pl.ds(pl.multiple_of(p * LANES, LANES), LANES)
            v = run[stable[2, 2 * p]] + run[stable[2, 2 * p + 1]]
            cumul, density = gelu_parts(v)
            out_ref[rows, lanes] = (v * cumul).astype(jnp.bfloat16)
            g[p, rows] = (up_ref[rows, lanes].astype(jnp.float32) * (cumul + v * density)).astype(jnp.bfloat16)
            if last:
                both = g[p].astype(jnp.float32).T.astype(jnp.bfloat16)
                gt[2 * p] = both[:TILE]
                gt[2 * p + 1] = both[TILE:]
            return carry

        lax.fori_loop(0, n_pair, gelu_pair, 0, unroll=UNROLL if n_pair % UNROLL == 0 else 1)

    def terms(b):
        for j in range(half):
            parts = []
            for i in (j, j + half):
                parts.append(jnp.dot(gt[sidc[b, 1, i]], xall[b * cap + i], preferred_element_type=jnp.float32))
            turned = jnp.concatenate(parts, axis=0).T
            dsend[b, j] = (turned[:TILE] + turned[TILE:]).astype(jnp.bfloat16)

    copy_up.wait()

    def early(c, carry):
        hidden(c, False)
        return carry

    lax.fori_loop(0, chunks - 1, early, 0)
    hidden(chunks - 1, True)

    odd_core = lax.rem(col, 2)
    mate = 1 + odd_core * (n_col - 2)

    def send_terms(i, carry):
        k = 2 - odd_core + i
        k = k + (i + 1) // (n_col - 1) * (mate - k)
        terms(at_col(k))
        d_col(k, col).start()
        return carry

    lax.fori_loop(0, n_col - 1, send_terms, 0)
    terms(col)
    for k in range(1, n_col):
        d_col(k, at_col(k)).wait_recv()
    own_count = cnt_ref[0]
    for j in range(half):
        total = dsend[col, j].astype(jnp.float32)
        for k in range(1, n_col):
            total = total + drecv[at_col(k), j].astype(jnp.float32)
        mixed[...] = jnp.where(lane_half * half + j < own_count, total, 0.0)
        one, two = mixed[even, :], mixed[odd, :]
        natural[j] = jnp.where(low, one, pltpu.roll(two, TILE, 1))
        natural[j + half] = jnp.where(low, pltpu.roll(one, TILE, 1), two)
    for j in range(TILE // 2):
        grad_ref[:, j * LANES : (j + 1) * LANES] = natural[:, j, :].astype(jnp.bfloat16)

    for c in range(chunks):
        for k in range(1, group):
            x_group(c, k, x).wait_send()
        for k in range(1, line):
            x_line(c, k, z).wait_send()
    for k in range(1, line):
        ids_line(k, z).wait_send()
    for k in range(1, n_col):
        ids_col(k, col).wait_send()
        w_col(k, col).wait_send()
        d_col(k, col).wait_send()


def body(activations, weight_tiles, tile_ids, tile_counts, upstream):
    n_row, n_col = lax.axis_size("row"), lax.axis_size("col")
    group = n_row // n_col
    tok, own_width = activations.shape
    ff_local = upstream.shape[1]
    per_col = ff_local // TILE
    cap = weight_tiles.shape[2]
    half = cap // 2
    slots = n_col * cap
    own_tiles = own_width // TILE
    tc = tok // CHUNKS
    rows = tc // 2
    width = -(-max(slots, per_col) // LANES) * LANES
    w = weight_tiles.reshape(cap, TILE * TILE)
    bf16, f32, i32 = jnp.bfloat16, jnp.float32, jnp.int32
    vmem = pl.BlockSpec(memory_space=pltpu.VMEM)
    smem = pl.BlockSpec(memory_space=pltpu.SMEM)
    hbm = pl.BlockSpec(memory_space=pltpu.HBM)
    dma = pltpu.SemaphoreType.DMA
    in_hbm = functools.partial(pltpu.with_memory_space_constraint, memory_space=pltpu.HBM)
    n_pair = ff_local // LANES
    output, grad = pl.pallas_call(
        functools.partial(kernel, n_row, n_col, per_col),
        out_shape=(
            jax.ShapeDtypeStruct((tok, ff_local), bf16),
            jax.ShapeDtypeStruct((cap, TILE * TILE), bf16),
        ),
        in_specs=[hbm, hbm, hbm, smem, hbm],
        out_specs=(vmem, vmem),
        scratch_shapes=[
            *[pltpu.VMEM((group * own_tiles, rows, LANES), bf16) for _ in range(CHUNKS)],
            pltpu.SMEM((cap,), i32),
            pltpu.VMEM(activations.shape, bf16),
            pltpu.VMEM(upstream.shape, bf16),
            pltpu.VMEM(w.shape, bf16),
            pltpu.VMEM((cap, TILE // 2, LANES), f32),
            pltpu.VMEM((TILE, LANES), f32),
            pltpu.VMEM((half, TILE, LANES), bf16),
            pltpu.VMEM((CHUNKS, n_col, cap, rows, LANES), bf16),
            pltpu.VMEM((CHUNKS, n_col, cap, rows, LANES), bf16),
            pltpu.VMEM((n_col, half, TILE, LANES), bf16),
            pltpu.VMEM((slots, 2 * TILE, LANES), bf16),
            pltpu.VMEM((slots, tok, LANES), bf16),
            pltpu.VMEM((8, LANES), i32),
            pltpu.VMEM((n_col, 8, LANES), i32),
            pltpu.VMEM((n_col, 8, LANES), i32),
            pltpu.SMEM((n_col, 8, LANES), i32),
            pltpu.SMEM((n_col, 8, LANES), i32),
            pltpu.VMEM((8, width), i32),
            pltpu.SMEM((8, width), i32),
            pltpu.VMEM((slots, tc, LANES), f32),
            pltpu.VMEM((slots + 1, tc, LANES), f32),
            pltpu.VMEM((n_pair, tok, LANES), bf16),
            pltpu.VMEM((per_col, TILE, tok), bf16),
            pltpu.VMEM((n_col, half, TILE, LANES), bf16),
            pltpu.VMEM((n_col, half, TILE, LANES), bf16),
            dma((CHUNKS, group)), dma((CHUNKS, group)),
            dma((n_col,)), dma((n_col,)),
            dma((n_col,)), dma((n_col,)),
            dma((n_col,)), dma((n_col,)),
            dma((CHUNKS, n_col)), dma((CHUNKS, n_col)),
            dma((n_col,)), dma((n_col,)),
            dma((5 + CHUNKS,)),
        ],
        compiler_params=pltpu.CompilerParams(
            collective_id=0, has_side_effects=True, vmem_limit_bytes=48 * 1024 * 1024
        ),
    )(in_hbm(activations), in_hbm(w), in_hbm(tile_ids.reshape(cap)), tile_counts.reshape(1), in_hbm(upstream))
    return (output, grad.reshape(1, 1, cap, TILE * TILE))


def solution(mesh):
    return jax.shard_map(
        body,
        mesh=mesh,
        in_specs=(
            P("col", "row"),
            P("col", "row", None, None),
            P("col", "row", None),
            P("col", "row"),
            P("col", "row"),
        ),
        out_specs=(P("col", "row"), P("col", "row", None, None)),
        check_vma=False,
    )
```

```python
import functools

import jax
import jax.numpy as jnp
from jax import lax
from jax.experimental import pallas as pl
from jax.experimental.pallas import tpu as pltpu
from jax.sharding import PartitionSpec as P

TILE = 64
LANES = 128
CHUNKS = 4
UNROLL = 6
MESH = pl.DeviceIdType.MESH


def gelu_parts(pre):
    cumul = 0.5 * (1.0 + lax.erf(pre * 0.7071067811865476))
    density = jnp.exp(-0.5 * pre * pre) * 0.3989422804014327
    return (cumul, density)


def kernel(
    n_row, n_col, per_col,
    x_hbm, w_hbm, ids_hbm, cnt_ref, up_hbm, out_ref, grad_ref, *scratch,
):
    xg, scratch = scratch[:CHUNKS], scratch[CHUNKS:]
    (
        ids_ref, x_ref, up_ref, w_ref, natural, mixed, wsrc, sendx, recvx, wbuf, wpl, xall, idsrc, idq, idc, sidq, sidc, table, stable,
        prod, run, g, gt, dsend, drecv,
        xg_s, xg_r, ic_s, ic_r, iq_s, iq_r, w_s, w_r, xz_s, xz_r, d_s, d_r, loc,
    ) = scratch
    cap = ids_hbm.shape[0]
    half = cap // 2
    slots = n_col * cap
    group = n_row // n_col
    line = n_col
    chunks = len(xg)
    all_tiles, packed_rows, _ = xg[0].shape
    tc = 2 * packed_rows
    own_tiles = all_tiles // group
    n_pair = g.shape[0]
    col = lax.axis_index("col")
    row = lax.axis_index("row")
    z = row // group
    x = lax.rem(row, group)

    def member(k):
        return lax.rem(x + k, group)

    def at_line(k):
        return lax.rem(z + k, line)

    def at_col(k):
        return lax.rem(col + k, n_col)

    copy_ids = pltpu.make_async_copy(ids_hbm, ids_ref, loc.at[0])
    copy_x = [
        pltpu.make_async_copy(x_hbm.at[pl.ds(c * tc, tc)], x_ref.at[pl.ds(c * tc, tc)], loc.at[5 + c])
        for c in range(chunks)
    ]
    copy_up = pltpu.make_async_copy(up_hbm, up_ref, loc.at[3])
    copy_ids.start()
    for copy in copy_x:
        copy.start()
    copy_w = pltpu.make_async_copy(w_hbm, w_ref, loc.at[4])
    copy_w.start()
    copy_up.start()
    barrier = pltpu.get_barrier_semaphore()
    for k in range(1, group):
        pl.semaphore_signal(barrier, inc=1, device_id={"row": z * group + member(k)}, device_id_type=MESH)
    for k in range(1, line):
        pl.semaphore_signal(barrier, inc=1, device_id={"row": at_line(k) * group + x}, device_id_type=MESH)
    for k in range(1, n_col):
        pl.semaphore_signal(barrier, inc=1, device_id={"col": at_col(k)}, device_id_type=MESH)

    lane8 = lax.broadcasted_iota(jnp.int32, (8, LANES), 1)
    row8 = lax.broadcasted_iota(jnp.int32, (8, LANES), 0)
    ids = jnp.zeros((8, LANES), jnp.int32)
    copy_ids.wait()
    for s in range(cap):
        ids = jnp.where(lane8 == s, ids_ref[s], ids)
    feature = ids // per_col
    hidden_tile = ids - feature * per_col
    packed = jnp.where(row8 == 0, feature, jnp.where(row8 == 1, hidden_tile, lax.rem(hidden_tile, 2)))
    packed = jnp.where(lane8 == cap, cnt_ref[0], packed)
    idsrc[...] = packed
    idc[col] = packed

    def pack(c):
        copy_x[c].wait()
        for t in range(own_tiles):
            lanes = slice(t * TILE, (t + 1) * TILE)
            top = x_ref[c * tc : c * tc + packed_rows, lanes].astype(jnp.float32)
            bottom = x_ref[c * tc + packed_rows : (c + 1) * tc, lanes].astype(jnp.float32)
            xg[c][x * own_tiles + t] = jnp.concatenate([top, bottom], axis=1).astype(jnp.bfloat16)

    pack(0)
    pl.semaphore_wait(barrier, group + line + n_col - 3)

    def remote(src, dst, send, recv, target):
        return pltpu.make_async_remote_copy(
            src_ref=src, dst_ref=dst, send_sem=send, recv_sem=recv, device_id=target, device_id_type=MESH
        )

    def ids_col(k, owner):
        return remote(idsrc, idc.at[owner], ic_s.at[k], ic_r.at[owner], {"col": at_col(k)})

    def ids_line(k, owner):
        to = at_line(k)
        return remote(idc.at[to], idq.at[owner], iq_s.at[k], iq_r.at[owner], {"row": to * group + x})

    def w_col(k, owner):
        return remote(wsrc, wbuf.at[owner], w_s.at[k], w_r.at[owner], {"col": at_col(k)})

    def x_group(c, k, owner):
        mine = xg[c].at[pl.ds(x * own_tiles, own_tiles)]
        theirs = xg[c].at[pl.ds(owner * own_tiles, own_tiles)]
        return remote(mine, theirs, xg_s.at[c, k], xg_r.at[c, owner], {"row": z * group + member(k)})

    def x_line(c, k, owner):
        to = at_line(k)
        return remote(
            sendx.at[c, to], recvx.at[c, owner], xz_s.at[c, k], xz_r.at[c, owner], {"row": to * group + x}
        )

    def d_col(k, owner):
        to = at_col(k)
        return remote(dsend.at[to], drecv.at[owner], d_s.at[k], d_r.at[owner], {"col": to})

    for k in range(1, n_col):
        ids_col(k, col).start()
    for k in range(1, group):
        x_group(0, k, x).start()

    def swap(c):
        pack(c)
        for k in range(1, group):
            x_group(c, k, x).start()

    if chunks > 1:
        swap(1)
    for k in range(1, n_col):
        ids_col(k, at_col(k)).wait_recv()
    for k in range(1, line):
        ids_line(k, z).start()
    idq[z] = idc[z]
    copy_c = pltpu.make_async_copy(idc, sidc, loc.at[1])
    copy_c.start()

    for c in range(2, chunks):
        swap(c)
    for k in range(1, line):
        ids_line(k, at_line(k)).wait_recv()
    copy_q = pltpu.make_async_copy(idq, sidq, loc.at[0])
    copy_q.start()
    copy_c.wait()
    copy_q.wait()

    def send_chunk(c):
        for k in range(1, group):
            x_group(c, k, member(k)).wait_recv()
        for k in range(line - 1, 0, -1):
            to = at_line(k)
            for s in range(cap):
                sendx[c, to, s] = xg[c][sidq[to, 0, s]]
            x_line(c, k, z).start()
        for s in range(cap):
            recvx[c, z, s] = xg[c][sidq[z, 0, s]]

    send_chunk(0)

    lane_half = lax.broadcasted_iota(jnp.int32, (TILE, LANES), 1) // TILE
    low = lax.broadcasted_iota(jnp.int32, (TILE // 2, LANES), 1) < TILE
    even, odd = pl.ds(0, TILE // 2, stride=2), pl.ds(1, TILE // 2, stride=2)
    copy_w.wait()
    for j in range(TILE // 2):
        natural[:, j, :] = w_ref[:, j * LANES : (j + 1) * LANES].astype(jnp.float32)
    for j in range(half):
        one, two = natural[j], natural[j + half]
        mixed[even, :] = jnp.where(low, one, pltpu.roll(two, TILE, 1))
        mixed[odd, :] = jnp.where(low, pltpu.roll(one, TILE, 1), two)
        wsrc[j] = mixed[...].astype(jnp.bfloat16)
    wbuf[col] = wsrc[...]
    for k in range(1, n_col):
        w_col(k, col).start()

    for c in range(1, chunks):
        send_chunk(c)

    width = table.shape[1]
    lanes_s = lax.broadcasted_iota(jnp.int32, (slots, width), 1)
    rows_s = lax.broadcasted_iota(jnp.int32, (slots, width), 0)
    key_row = jnp.full((1, width), per_col + 1, jnp.int32) * slots + slots
    key_col = jnp.zeros((slots, width), jnp.int32)
    lane1 = lax.broadcasted_iota(jnp.int32, (1, width), 1)
    for s in range(slots):
        b, j = s // cap, s % cap
        f = jnp.where(j < sidc[b, 0, cap], sidc[b, 1, j], per_col)
        key_row = jnp.where(lane1 == s, f * slots + s, key_row)
        key_col = jnp.where(rows_s == s, f, key_col)
    ahead = jnp.where(key_row < key_col * slots + rows_s, 1, 0)
    rank = jnp.sum(ahead, axis=1, keepdims=True)
    here = jnp.where(rank == lanes_s, 1, 0)
    table[0:1, :] = jnp.sum(here * rows_s, axis=0, keepdims=True)
    table[1:2, :] = jnp.sum(here * key_col, axis=0, keepdims=True)
    upto = jnp.sum(jnp.where(key_col <= lanes_s, 1, 0), axis=0, keepdims=True)
    some = jnp.sum(jnp.where(key_col == lanes_s, 1, 0), axis=0, keepdims=True)
    table[2:3, :] = jnp.where(some > 0, upto - 1, slots)
    table[3:8, :] = jnp.zeros((5, width), jnp.int32)
    copy_t = pltpu.make_async_copy(table, stable, loc.at[0])
    copy_t.start()
    copy_t.wait()

    for k in range(1, n_col):
        w_col(k, at_col(k)).wait_recv()

    def place_weights(b, carry):
        for s in range(cap):
            side = sidc[b, 2, s]
            both = jnp.where(lane_half == s // half, wbuf[b, s % half].astype(jnp.float32), 0.0)
            both = both + pltpu.roll(both, TILE, 1)
            placed = jnp.where(lane_half == side, both, 0.0).astype(jnp.bfloat16)
            wpl[b * cap + s, :TILE] = placed
            wpl[b * cap + s, TILE:] = placed
        return carry

    lax.fori_loop(0, n_col, place_weights, 0)
    run[slots] = jnp.zeros((tc, LANES), jnp.float32)

    packed_half = lax.broadcasted_iota(jnp.int32, (packed_rows, LANES), 1) // TILE
    first = jnp.where(packed_half == 0, 1.0, 0.0).astype(jnp.bfloat16)
    second = jnp.where(packed_half == 1, 1.0, 0.0).astype(jnp.bfloat16)

    def chunk_rows(c):
        return pl.ds(pl.multiple_of(c * tc, tc), tc)

    def products(c, b):
        for s in range(cap):
            tile = recvx[c, b, s]
            spread = jnp.concatenate([tile * first, tile * second], axis=0)
            xall[b * cap + s, chunk_rows(c)] = spread
            prod[b * cap + s] = jnp.dot(spread, wpl[b * cap + s], preferred_element_type=jnp.float32)

    def hidden(c, last):
        products(c, z)

        def later(k, carry):
            b = at_line(k)
            x_line(c, k, b).wait_recv()
            products(c, b)
            return carry

        lax.fori_loop(1, line, later, 0)

        def add_run(r, held):
            same = jnp.where(stable[1, r] == stable[1, jnp.maximum(r - 1, 0)], 1.0, 0.0)
            total = prod[stable[0, r]] + held * same
            run[r] = total
            return total

        lax.fori_loop(0, slots, add_run, jnp.zeros((tc, LANES), jnp.float32), unroll=12 if slots % 12 == 0 else 1)

        rows = chunk_rows(c)

        def gelu_pair(p, carry):
            lanes = pl.ds(pl.multiple_of(p * LANES, LANES), LANES)
            v = run[stable[2, 2 * p]] + run[stable[2, 2 * p + 1]]
            cumul, density = gelu_parts(v)
            out_ref[rows, lanes] = (v * cumul).astype(jnp.bfloat16)
            g[p, rows] = (up_ref[rows, lanes].astype(jnp.float32) * (cumul + v * density)).astype(jnp.bfloat16)
            if last:
                both = g[p].astype(jnp.float32).T.astype(jnp.bfloat16)
                gt[2 * p] = both[:TILE]
                gt[2 * p + 1] = both[TILE:]
            return carry

        lax.fori_loop(0, n_pair, gelu_pair, 0, unroll=UNROLL if n_pair % UNROLL == 0 else 1)

    def terms(b):
        for j in range(half):
            parts = []
            for i in (j, j + half):
                parts.append(jnp.dot(gt[sidc[b, 1, i]], xall[b * cap + i], preferred_element_type=jnp.float32))
            turned = jnp.concatenate(parts, axis=0).T
            dsend[b, j] = (turned[:TILE] + turned[TILE:]).astype(jnp.bfloat16)

    copy_up.wait()

    def early(c, carry):
        hidden(c, False)
        return carry

    lax.fori_loop(0, chunks - 1, early, 0)
    hidden(chunks - 1, True)

    odd_core = lax.rem(col, 2)
    mate = 1 + odd_core * (n_col - 2)

    def send_terms(i, carry):
        k = 2 - odd_core + i
        k = k + (i + 1) // (n_col - 1) * (mate - k)
        terms(at_col(k))
        d_col(k, col).start()
        return carry

    if n_col <= 4:
        for i in range(n_col - 1):
            send_terms(i, 0)
    else:
        lax.fori_loop(0, n_col - 1, send_terms, 0)
    terms(col)
    for k in range(1, n_col):
        d_col(k, at_col(k)).wait_recv()
    own_count = cnt_ref[0]
    for j in range(half):
        total = dsend[col, j].astype(jnp.float32)
        for k in range(1, n_col):
            total = total + drecv[at_col(k), j].astype(jnp.float32)
        mixed[...] = jnp.where(lane_half * half + j < own_count, total, 0.0)
        one, two = mixed[even, :], mixed[odd, :]
        natural[j] = jnp.where(low, one, pltpu.roll(two, TILE, 1))
        natural[j + half] = jnp.where(low, pltpu.roll(one, TILE, 1), two)
    for j in range(TILE // 2):
        grad_ref[:, j * LANES : (j + 1) * LANES] = natural[:, j, :].astype(jnp.bfloat16)

    for c in range(chunks):
        for k in range(1, group):
            x_group(c, k, x).wait_send()
        for k in range(1, line):
            x_line(c, k, z).wait_send()
    for k in range(1, line):
        ids_line(k, z).wait_send()
    for k in range(1, n_col):
        ids_col(k, col).wait_send()
        w_col(k, col).wait_send()
        d_col(k, col).wait_send()


def body(activations, weight_tiles, tile_ids, tile_counts, upstream):
    n_row, n_col = lax.axis_size("row"), lax.axis_size("col")
    group = n_row // n_col
    tok, own_width = activations.shape
    ff_local = upstream.shape[1]
    per_col = ff_local // TILE
    cap = weight_tiles.shape[2]
    half = cap // 2
    slots = n_col * cap
    own_tiles = own_width // TILE
    tc = tok // CHUNKS
    rows = tc // 2
    width = -(-max(slots, per_col) // LANES) * LANES
    w = weight_tiles.reshape(cap, TILE * TILE)
    bf16, f32, i32 = jnp.bfloat16, jnp.float32, jnp.int32
    vmem = pl.BlockSpec(memory_space=pltpu.VMEM)
    smem = pl.BlockSpec(memory_space=pltpu.SMEM)
    hbm = pl.BlockSpec(memory_space=pltpu.HBM)
    dma = pltpu.SemaphoreType.DMA
    in_hbm = functools.partial(pltpu.with_memory_space_constraint, memory_space=pltpu.HBM)
    n_pair = ff_local // LANES
    output, grad = pl.pallas_call(
        functools.partial(kernel, n_row, n_col, per_col),
        out_shape=(
            jax.ShapeDtypeStruct((tok, ff_local), bf16),
            jax.ShapeDtypeStruct((cap, TILE * TILE), bf16),
        ),
        in_specs=[hbm, hbm, hbm, smem, hbm],
        out_specs=(vmem, vmem),
        scratch_shapes=[
            *[pltpu.VMEM((group * own_tiles, rows, LANES), bf16) for _ in range(CHUNKS)],
            pltpu.SMEM((cap,), i32),
            pltpu.VMEM(activations.shape, bf16),
            pltpu.VMEM(upstream.shape, bf16),
            pltpu.VMEM(w.shape, bf16),
            pltpu.VMEM((cap, TILE // 2, LANES), f32),
            pltpu.VMEM((TILE, LANES), f32),
            pltpu.VMEM((half, TILE, LANES), bf16),
            pltpu.VMEM((CHUNKS, n_col, cap, rows, LANES), bf16),
            pltpu.VMEM((CHUNKS, n_col, cap, rows, LANES), bf16),
            pltpu.VMEM((n_col, half, TILE, LANES), bf16),
            pltpu.VMEM((slots, 2 * TILE, LANES), bf16),
            pltpu.VMEM((slots, tok, LANES), bf16),
            pltpu.VMEM((8, LANES), i32),
            pltpu.VMEM((n_col, 8, LANES), i32),
            pltpu.VMEM((n_col, 8, LANES), i32),
            pltpu.SMEM((n_col, 8, LANES), i32),
            pltpu.SMEM((n_col, 8, LANES), i32),
            pltpu.VMEM((8, width), i32),
            pltpu.SMEM((8, width), i32),
            pltpu.VMEM((slots, tc, LANES), f32),
            pltpu.VMEM((slots + 1, tc, LANES), f32),
            pltpu.VMEM((n_pair, tok, LANES), bf16),
            pltpu.VMEM((per_col, TILE, tok), bf16),
            pltpu.VMEM((n_col, half, TILE, LANES), bf16),
            pltpu.VMEM((n_col, half, TILE, LANES), bf16),
            dma((CHUNKS, group)), dma((CHUNKS, group)),
            dma((n_col,)), dma((n_col,)),
            dma((n_col,)), dma((n_col,)),
            dma((n_col,)), dma((n_col,)),
            dma((CHUNKS, n_col)), dma((CHUNKS, n_col)),
            dma((n_col,)), dma((n_col,)),
            dma((5 + CHUNKS,)),
        ],
        compiler_params=pltpu.CompilerParams(
            collective_id=0, has_side_effects=True, vmem_limit_bytes=48 * 1024 * 1024
        ),
    )(in_hbm(activations), in_hbm(w), in_hbm(tile_ids.reshape(cap)), tile_counts.reshape(1), in_hbm(upstream))
    return (output, grad.reshape(1, 1, cap, TILE * TILE))


def solution(mesh):
    return jax.shard_map(
        body,
        mesh=mesh,
        in_specs=(
            P("col", "row"),
            P("col", "row", None, None),
            P("col", "row", None),
            P("col", "row"),
            P("col", "row"),
        ),
        out_specs=(P("col", "row"), P("col", "row", None, None)),
        check_vma=False,
    )
```

```python
import functools

import jax
import jax.numpy as jnp
from jax import lax
from jax.experimental import pallas as pl
from jax.experimental.pallas import tpu as pltpu
from jax.sharding import PartitionSpec as P

TILE = 64
LANES = 128
CHUNKS = 4
UNROLL = 6
MESH = pl.DeviceIdType.MESH


def gelu_parts(pre):
    cumul = 0.5 * (1.0 + lax.erf(pre * 0.7071067811865476))
    density = jnp.exp(-0.5 * pre * pre) * 0.3989422804014327
    return (cumul, density)


def kernel(
    n_row, n_col, per_col,
    x_hbm, w_hbm, ids_hbm, cnt_ref, up_hbm, out_ref, grad_ref, *scratch,
):
    xg, scratch = scratch[:CHUNKS], scratch[CHUNKS:]
    (
        ids_ref, x_ref, up_ref, w_ref, natural, mixed, wsrc, sendx, recvx, wbuf, wpl, xall, idsrc, idq, idc, sidq, sidc, table, stable,
        prod, run, g, gt, dsend, drecv,
        xg_s, xg_r, ic_s, ic_r, iq_s, iq_r, w_s, w_r, xz_s, xz_r, d_s, d_r, loc,
    ) = scratch
    cap = ids_hbm.shape[0]
    half = cap // 2
    slots = n_col * cap
    group = n_row // n_col
    line = n_col
    chunks = len(xg)
    all_tiles, packed_rows, _ = xg[0].shape
    tc = 2 * packed_rows
    own_tiles = all_tiles // group
    n_pair = g.shape[0]
    col = lax.axis_index("col")
    row = lax.axis_index("row")
    z = row // group
    x = lax.rem(row, group)

    def member(k):
        return lax.rem(x + k, group)

    def at_line(k):
        return lax.rem(z + k, line)

    def at_col(k):
        return lax.rem(col + k, n_col)

    copy_ids = pltpu.make_async_copy(ids_hbm, ids_ref, loc.at[0])
    copy_x = [
        pltpu.make_async_copy(x_hbm.at[pl.ds(c * tc, tc)], x_ref.at[pl.ds(c * tc, tc)], loc.at[5 + c])
        for c in range(chunks)
    ]
    copy_up = pltpu.make_async_copy(up_hbm, up_ref, loc.at[3])
    copy_ids.start()
    for copy in copy_x:
        copy.start()
    copy_w = pltpu.make_async_copy(w_hbm, w_ref, loc.at[4])
    copy_w.start()
    copy_up.start()
    barrier = pltpu.get_barrier_semaphore()
    for k in range(1, group):
        pl.semaphore_signal(barrier, inc=1, device_id={"row": z * group + member(k)}, device_id_type=MESH)
    for k in range(1, line):
        pl.semaphore_signal(barrier, inc=1, device_id={"row": at_line(k) * group + x}, device_id_type=MESH)
    for k in range(1, n_col):
        pl.semaphore_signal(barrier, inc=1, device_id={"col": at_col(k)}, device_id_type=MESH)

    lane8 = lax.broadcasted_iota(jnp.int32, (8, LANES), 1)
    row8 = lax.broadcasted_iota(jnp.int32, (8, LANES), 0)
    ids = jnp.zeros((8, LANES), jnp.int32)
    copy_ids.wait()
    for s in range(cap):
        ids = jnp.where(lane8 == s, ids_ref[s], ids)
    feature = ids // per_col
    hidden_tile = ids - feature * per_col
    packed = jnp.where(row8 == 0, feature, jnp.where(row8 == 1, hidden_tile, lax.rem(hidden_tile, 2)))
    packed = jnp.where(lane8 == cap, cnt_ref[0], packed)
    idsrc[...] = packed
    idc[col] = packed

    def pack(c):
        copy_x[c].wait()
        for t in range(own_tiles):
            lanes = slice(t * TILE, (t + 1) * TILE)
            top = x_ref[c * tc : c * tc + packed_rows, lanes].astype(jnp.float32)
            bottom = x_ref[c * tc + packed_rows : (c + 1) * tc, lanes].astype(jnp.float32)
            xg[c][x * own_tiles + t] = jnp.concatenate([top, bottom], axis=1).astype(jnp.bfloat16)

    pl.semaphore_wait(barrier, group + line + n_col - 3)

    def remote(src, dst, send, recv, target):
        return pltpu.make_async_remote_copy(
            src_ref=src, dst_ref=dst, send_sem=send, recv_sem=recv, device_id=target, device_id_type=MESH
        )

    def ids_col(k, owner):
        return remote(idsrc, idc.at[owner], ic_s.at[k], ic_r.at[owner], {"col": at_col(k)})

    def ids_line(k, owner):
        to = at_line(k)
        return remote(idc.at[to], idq.at[owner], iq_s.at[k], iq_r.at[owner], {"row": to * group + x})

    def w_col(k, owner):
        return remote(wsrc, wbuf.at[owner], w_s.at[k], w_r.at[owner], {"col": at_col(k)})

    def x_group(c, k, owner):
        mine = xg[c].at[pl.ds(x * own_tiles, own_tiles)]
        theirs = xg[c].at[pl.ds(owner * own_tiles, own_tiles)]
        return remote(mine, theirs, xg_s.at[c, k], xg_r.at[c, owner], {"row": z * group + member(k)})

    def x_line(c, k, owner):
        to = at_line(k)
        return remote(
            sendx.at[c, to], recvx.at[c, owner], xz_s.at[c, k], xz_r.at[c, owner], {"row": to * group + x}
        )

    def d_col(k, owner):
        to = at_col(k)
        return remote(dsend.at[to], drecv.at[owner], d_s.at[k], d_r.at[owner], {"col": to})

    for k in range(1, n_col):
        ids_col(k, col).start()
    pack(0)
    for k in range(1, group):
        x_group(0, k, x).start()

    def swap(c):
        pack(c)
        for k in range(1, group):
            x_group(c, k, x).start()

    if chunks > 1:
        swap(1)
    for k in range(1, n_col):
        ids_col(k, at_col(k)).wait_recv()
    for k in range(1, line):
        ids_line(k, z).start()
    idq[z] = idc[z]
    copy_c = pltpu.make_async_copy(idc, sidc, loc.at[1])
    copy_c.start()

    for c in range(2, chunks):
        swap(c)
    for k in range(1, line):
        ids_line(k, at_line(k)).wait_recv()
    copy_q = pltpu.make_async_copy(idq, sidq, loc.at[0])
    copy_q.start()
    copy_c.wait()
    copy_q.wait()

    def send_chunk(c):
        for k in range(1, group):
            x_group(c, k, member(k)).wait_recv()
        for k in range(line - 1, 0, -1):
            to = at_line(k)
            for s in range(cap):
                sendx[c, to, s] = xg[c][sidq[to, 0, s]]
            x_line(c, k, z).start()
        for s in range(cap):
            recvx[c, z, s] = xg[c][sidq[z, 0, s]]

    send_chunk(0)

    lane_half = lax.broadcasted_iota(jnp.int32, (TILE, LANES), 1) // TILE
    low = lax.broadcasted_iota(jnp.int32, (TILE // 2, LANES), 1) < TILE
    even, odd = pl.ds(0, TILE // 2, stride=2), pl.ds(1, TILE // 2, stride=2)
    copy_w.wait()
    for j in range(TILE // 2):
        natural[:, j, :] = w_ref[:, j * LANES : (j + 1) * LANES].astype(jnp.float32)
    for j in range(half):
        one, two = natural[j], natural[j + half]
        mixed[even, :] = jnp.where(low, one, pltpu.roll(two, TILE, 1))
        mixed[odd, :] = jnp.where(low, pltpu.roll(one, TILE, 1), two)
        wsrc[j] = mixed[...].astype(jnp.bfloat16)
    wbuf[col] = wsrc[...]
    for k in range(1, n_col):
        w_col(k, col).start()

    for c in range(1, chunks):
        send_chunk(c)

    width = table.shape[1]
    lanes_s = lax.broadcasted_iota(jnp.int32, (slots, width), 1)
    rows_s = lax.broadcasted_iota(jnp.int32, (slots, width), 0)
    key_row = jnp.full((1, width), per_col + 1, jnp.int32) * slots + slots
    key_col = jnp.zeros((slots, width), jnp.int32)
    lane1 = lax.broadcasted_iota(jnp.int32, (1, width), 1)
    for s in range(slots):
        b, j = s // cap, s % cap
        f = jnp.where(j < sidc[b, 0, cap], sidc[b, 1, j], per_col)
        key_row = jnp.where(lane1 == s, f * slots + s, key_row)
        key_col = jnp.where(rows_s == s, f, key_col)
    ahead = jnp.where(key_row < key_col * slots + rows_s, 1, 0)
    rank = jnp.sum(ahead, axis=1, keepdims=True)
    here = jnp.where(rank == lanes_s, 1, 0)
    table[0:1, :] = jnp.sum(here * rows_s, axis=0, keepdims=True)
    table[1:2, :] = jnp.sum(here * key_col, axis=0, keepdims=True)
    upto = jnp.sum(jnp.where(key_col <= lanes_s, 1, 0), axis=0, keepdims=True)
    some = jnp.sum(jnp.where(key_col == lanes_s, 1, 0), axis=0, keepdims=True)
    table[2:3, :] = jnp.where(some > 0, upto - 1, slots)
    table[3:8, :] = jnp.zeros((5, width), jnp.int32)
    copy_t = pltpu.make_async_copy(table, stable, loc.at[0])
    copy_t.start()
    copy_t.wait()

    for k in range(1, n_col):
        w_col(k, at_col(k)).wait_recv()

    def place_weights(b, carry):
        for s in range(cap):
            side = sidc[b, 2, s]
            both = jnp.where(lane_half == s // half, wbuf[b, s % half].astype(jnp.float32), 0.0)
            both = both + pltpu.roll(both, TILE, 1)
            placed = jnp.where(lane_half == side, both, 0.0).astype(jnp.bfloat16)
            wpl[b * cap + s, :TILE] = placed
            wpl[b * cap + s, TILE:] = placed
        return carry

    lax.fori_loop(0, n_col, place_weights, 0)
    run[slots] = jnp.zeros((tc, LANES), jnp.float32)

    packed_half = lax.broadcasted_iota(jnp.int32, (packed_rows, LANES), 1) // TILE
    first = jnp.where(packed_half == 0, 1.0, 0.0).astype(jnp.bfloat16)
    second = jnp.where(packed_half == 1, 1.0, 0.0).astype(jnp.bfloat16)

    def chunk_rows(c):
        return pl.ds(pl.multiple_of(c * tc, tc), tc)

    def products(c, b):
        for s in range(cap):
            tile = recvx[c, b, s]
            spread = jnp.concatenate([tile * first, tile * second], axis=0)
            xall[b * cap + s, chunk_rows(c)] = spread
            prod[b * cap + s] = jnp.dot(spread, wpl[b * cap + s], preferred_element_type=jnp.float32)

    def hidden(c, last):
        products(c, z)

        def later(k, carry):
            b = at_line(k)
            x_line(c, k, b).wait_recv()
            products(c, b)
            return carry

        lax.fori_loop(1, line, later, 0)

        def add_run(r, held):
            same = jnp.where(stable[1, r] == stable[1, jnp.maximum(r - 1, 0)], 1.0, 0.0)
            total = prod[stable[0, r]] + held * same
            run[r] = total
            return total

        lax.fori_loop(0, slots, add_run, jnp.zeros((tc, LANES), jnp.float32), unroll=12 if slots % 12 == 0 else 1)

        rows = chunk_rows(c)

        def gelu_pair(p, carry):
            lanes = pl.ds(pl.multiple_of(p * LANES, LANES), LANES)
            v = run[stable[2, 2 * p]] + run[stable[2, 2 * p + 1]]
            cumul, density = gelu_parts(v)
            out_ref[rows, lanes] = (v * cumul).astype(jnp.bfloat16)
            g[p, rows] = (up_ref[rows, lanes].astype(jnp.float32) * (cumul + v * density)).astype(jnp.bfloat16)
            if last:
                both = g[p].astype(jnp.float32).T.astype(jnp.bfloat16)
                gt[2 * p] = both[:TILE]
                gt[2 * p + 1] = both[TILE:]
            return carry

        lax.fori_loop(0, n_pair, gelu_pair, 0, unroll=UNROLL if n_pair % UNROLL == 0 else 1)

    def terms(b):
        for j in range(half):
            parts = []
            for i in (j, j + half):
                parts.append(jnp.dot(gt[sidc[b, 1, i]], xall[b * cap + i], preferred_element_type=jnp.float32))
            turned = jnp.concatenate(parts, axis=0).T
            dsend[b, j] = (turned[:TILE] + turned[TILE:]).astype(jnp.bfloat16)

    copy_up.wait()

    def early(c, carry):
        hidden(c, False)
        return carry

    lax.fori_loop(0, chunks - 1, early, 0)
    hidden(chunks - 1, True)

    odd_core = lax.rem(col, 2)
    mate = 1 + odd_core * (n_col - 2)

    def send_terms(i, carry):
        k = 2 - odd_core + i
        k = k + (i + 1) // (n_col - 1) * (mate - k)
        terms(at_col(k))
        d_col(k, col).start()
        return carry

    if n_col <= 4:
        for i in range(n_col - 1):
            send_terms(i, 0)
    else:
        lax.fori_loop(0, n_col - 1, send_terms, 0)
    terms(col)
    for k in range(1, n_col):
        d_col(k, at_col(k)).wait_recv()
    own_count = cnt_ref[0]
    for j in range(half):
        total = dsend[col, j].astype(jnp.float32)
        for k in range(1, n_col):
            total = total + drecv[at_col(k), j].astype(jnp.float32)
        mixed[...] = jnp.where(lane_half * half + j < own_count, total, 0.0)
        one, two = mixed[even, :], mixed[odd, :]
        natural[j] = jnp.where(low, one, pltpu.roll(two, TILE, 1))
        natural[j + half] = jnp.where(low, pltpu.roll(one, TILE, 1), two)
    for j in range(TILE // 2):
        grad_ref[:, j * LANES : (j + 1) * LANES] = natural[:, j, :].astype(jnp.bfloat16)

    for c in range(chunks):
        for k in range(1, group):
            x_group(c, k, x).wait_send()
        for k in range(1, line):
            x_line(c, k, z).wait_send()
    for k in range(1, line):
        ids_line(k, z).wait_send()
    for k in range(1, n_col):
        ids_col(k, col).wait_send()
        w_col(k, col).wait_send()
        d_col(k, col).wait_send()


def body(activations, weight_tiles, tile_ids, tile_counts, upstream):
    n_row, n_col = lax.axis_size("row"), lax.axis_size("col")
    group = n_row // n_col
    tok, own_width = activations.shape
    ff_local = upstream.shape[1]
    per_col = ff_local // TILE
    cap = weight_tiles.shape[2]
    half = cap // 2
    slots = n_col * cap
    own_tiles = own_width // TILE
    tc = tok // CHUNKS
    rows = tc // 2
    width = -(-max(slots, per_col) // LANES) * LANES
    w = weight_tiles.reshape(cap, TILE * TILE)
    bf16, f32, i32 = jnp.bfloat16, jnp.float32, jnp.int32
    vmem = pl.BlockSpec(memory_space=pltpu.VMEM)
    smem = pl.BlockSpec(memory_space=pltpu.SMEM)
    hbm = pl.BlockSpec(memory_space=pltpu.HBM)
    dma = pltpu.SemaphoreType.DMA
    in_hbm = functools.partial(pltpu.with_memory_space_constraint, memory_space=pltpu.HBM)
    n_pair = ff_local // LANES
    output, grad = pl.pallas_call(
        functools.partial(kernel, n_row, n_col, per_col),
        out_shape=(
            jax.ShapeDtypeStruct((tok, ff_local), bf16),
            jax.ShapeDtypeStruct((cap, TILE * TILE), bf16),
        ),
        in_specs=[hbm, hbm, hbm, smem, hbm],
        out_specs=(vmem, vmem),
        scratch_shapes=[
            *[pltpu.VMEM((group * own_tiles, rows, LANES), bf16) for _ in range(CHUNKS)],
            pltpu.SMEM((cap,), i32),
            pltpu.VMEM(activations.shape, bf16),
            pltpu.VMEM(upstream.shape, bf16),
            pltpu.VMEM(w.shape, bf16),
            pltpu.VMEM((cap, TILE // 2, LANES), f32),
            pltpu.VMEM((TILE, LANES), f32),
            pltpu.VMEM((half, TILE, LANES), bf16),
            pltpu.VMEM((CHUNKS, n_col, cap, rows, LANES), bf16),
            pltpu.VMEM((CHUNKS, n_col, cap, rows, LANES), bf16),
            pltpu.VMEM((n_col, half, TILE, LANES), bf16),
            pltpu.VMEM((slots, 2 * TILE, LANES), bf16),
            pltpu.VMEM((slots, tok, LANES), bf16),
            pltpu.VMEM((8, LANES), i32),
            pltpu.VMEM((n_col, 8, LANES), i32),
            pltpu.VMEM((n_col, 8, LANES), i32),
            pltpu.SMEM((n_col, 8, LANES), i32),
            pltpu.SMEM((n_col, 8, LANES), i32),
            pltpu.VMEM((8, width), i32),
            pltpu.SMEM((8, width), i32),
            pltpu.VMEM((slots, tc, LANES), f32),
            pltpu.VMEM((slots + 1, tc, LANES), f32),
            pltpu.VMEM((n_pair, tok, LANES), bf16),
            pltpu.VMEM((per_col, TILE, tok), bf16),
            pltpu.VMEM((n_col, half, TILE, LANES), bf16),
            pltpu.VMEM((n_col, half, TILE, LANES), bf16),
            dma((CHUNKS, group)), dma((CHUNKS, group)),
            dma((n_col,)), dma((n_col,)),
            dma((n_col,)), dma((n_col,)),
            dma((n_col,)), dma((n_col,)),
            dma((CHUNKS, n_col)), dma((CHUNKS, n_col)),
            dma((n_col,)), dma((n_col,)),
            dma((5 + CHUNKS,)),
        ],
        compiler_params=pltpu.CompilerParams(
            collective_id=0, has_side_effects=True, vmem_limit_bytes=48 * 1024 * 1024
        ),
    )(in_hbm(activations), in_hbm(w), in_hbm(tile_ids.reshape(cap)), tile_counts.reshape(1), in_hbm(upstream))
    return (output, grad.reshape(1, 1, cap, TILE * TILE))


def solution(mesh):
    return jax.shard_map(
        body,
        mesh=mesh,
        in_specs=(
            P("col", "row"),
            P("col", "row", None, None),
            P("col", "row", None),
            P("col", "row"),
            P("col", "row"),
        ),
        out_specs=(P("col", "row"), P("col", "row", None, None)),
        check_vma=False,
    )
```
